256 devices in a mesh: row: 128 (over z, y, x), rhs: 2 (over core).
Axes of the slice: x: 4, y: 4, z: 8, core: 2. Of those that a mesh axis runs over, the one named last changes fastest.
Arguments:
- source_field: float32 [2, 48, 131072], P(None, 'rhs', 'row'), may hold values from -6 to 6
- near_blocks: bfloat16 [512, 4, 2, 256, 256], P('row'), may hold values from -0.125 to 0.125
- near_offsets: int32 [512, 4], P('row'), may hold values from -2 to 2, as said below
- far_v: bfloat16 [16384, 2, 24, 256], P('row'), may hold values from -0.25 to 0.25
- far_u: bfloat16 [16384, 2, 24, 256], P('row', None, None, 'rhs'), may hold values from -0.109375 to 0.109375
- far_rank: int32 [16384], P('row'), may hold values from 8 to 24
- far_col_local: int32 [16384], P('row'), may hold values from 0 to 3
- far_dest: int32 [16384, 1], P('row'), may hold values from 0 to 127; in each aligned block of 128 rows (0 to 127, 128 to 255, ...) at most 2 rows name the same one
- far_row_local: int32 [16384], P('row'), may hold values from 0 to 3
Outputs:
- result: float32 [2, 48, 131072], P(None, 'rhs', 'row')
The draws below stay inside these ranges and needn't reach their ends.
Inputs may be any that keep to these rules, and one draw needn't show every extreme that they name: `near_offsets`: offset 0 comes first for every cluster and a cluster's offsets are distinct; the first cluster of each index of row has an offset -2, the last one an offset 2. `far_dest`: among the 128 admissible blocks of one owner at most 2 name the same device; in every draw some owner has exactly 2 for one device.
All inputs are finite; a program needn't handle non-finite values.
Results may differ from the reference program's by a relative error of at most 0.011.
Values may be sent and summed in bfloat16 or wider, within the bound.
No kernel may reach another device: no remote copies, remote signals or barrier semaphores. Data moves between devices by JAX's collectives and lax.ppermute only.
A program may use at most 128 MiB of HBM per device.

```python
import math
import jax
import jax.numpy as jnp
import numpy as np
from jax import lax

LEAF = 256
RANK = 24
NRHS = 48
NEAR = 4
APPS = 4
CL_DEV = 4
FAR_DEV = 128
WIN = 2
CAP = 2
CLUSTERS = 512
PANELS = 131072
FAR_TOTAL = 16384
N_ROW = 128


def draw_near_offsets(key, part):
    keys = jax.random.split(key, CLUSTERS)
    cluster_ids = jnp.arange(CLUSTERS, dtype=jnp.int32)
    position = cluster_ids % CL_DEV
    target = jnp.where(position == 0, 0, jnp.where(position == CL_DEV - 1, 2 * WIN - 1, -1)).astype(jnp.int32)

    def per_cluster(one_key, wanted):
        shuffled = jax.random.permutation(one_key, 2 * WIN).astype(jnp.int32)
        swapped = jnp.where(shuffled == wanted, shuffled[0], shuffled)
        swapped = swapped.at[0].set(jnp.where(wanted >= 0, wanted, shuffled[0]))
        offsets = swapped - WIN + (swapped >= WIN).astype(jnp.int32)
        return jnp.concatenate([jnp.zeros((1,), jnp.int32), offsets[:NEAR - 1]])
    return jax.vmap(per_cluster)(keys, target).astype(jnp.int32)


def plant(drawn, own_key, smallest, top_value):
    extent = drawn.shape
    index_at = [jax.random.randint(jax.random.fold_in(own_key, axis), (), 0, extent[axis]) for axis in range(len(extent))]
    drawn = drawn.at[tuple(index_at)].set(smallest)
    longest = extent.index(max(extent))
    index_at[longest] = (index_at[longest] + 1) % extent[longest]
    return drawn.at[tuple(index_at)].set(top_value)


def shard_levels(rng, dims, pieces, low, high):
    def one(axis_at, parts):
        steps = jax.random.uniform(jax.random.fold_in(jax.random.fold_in(rng, 6), axis_at), (parts,), jnp.float32, low / len(pieces), high / len(pieces))
        return jnp.repeat(jnp.exp(steps), dims[axis_at] // parts).reshape((-1,) + (1,) * (len(dims) - axis_at - 1))

    gain = one(*pieces[0])
    for cut in pieces[1:]:
        gain = gain * one(*cut)
    return gain


def routed_block(rng, own, number, rows, count, top, most, slope):
    sequence = jax.random.permutation(rng, count)
    packed, common = shares(count, rows * top, most, slope, True), shares(count, rows * top, most, slope, False)
    places = jnp.arange(count)

    def named(sizes, rotation):
        used = int((sizes > 0).sum())
        fixed = max(1, used // 4)
        passed = fixed + (places - fixed + rotation * (used - fixed)) % max(1, count - fixed)
        return jnp.zeros((count,), jnp.int32).at[sequence[jnp.where(places < fixed, places, passed)]].set(jnp.asarray(sizes, jnp.int32))

    sizes = jnp.where(number % 4 == 0, named(packed, number // 4), named(common, number - number // 4 - 1))
    mixed = jax.random.permutation(jax.random.fold_in(own, 3), count)
    donor, taker = mixed[0:count // 2 * 2:2], mixed[1:count // 2 * 2:2]
    slack = jnp.minimum(sizes[donor] - 1, most - sizes[taker]) // 2
    slack = jnp.where((donor == sequence[0]) | (taker == sequence[0]) | (sizes[taker] == 0), 0, jnp.maximum(slack, 0))
    passed = jax.random.randint(jax.random.fold_in(own, 4), (count // 2,), 0, 1 << 20) % (slack + 1)
    sizes = sizes.at[donor].add(-passed).at[taker].add(passed)
    labels = jnp.searchsorted(jnp.cumsum(sizes), jnp.arange(rows * top), side="right").astype(jnp.int32)
    listing = labels.reshape(top, rows).T
    listing = listing[jax.random.permutation(jax.random.fold_in(own, 1), rows)]
    rotation = jax.random.randint(jax.random.fold_in(own, 2), (rows, 1), 0, top)
    return jnp.take_along_axis(listing, (jnp.arange(top)[None, :] + rotation) % top, axis=1)


def shares(number_of, total, reach, skew, full):
    weights = [(1 << 20) // math.isqrt(grade ** skew) + 1 for grade in range(1, number_of + 1)]
    largest = reach if full else min(reach, max(-(-total // number_of), total * weights[0] // sum(weights)))
    least = 1 if total - largest >= number_of - 1 else 0
    counts, rest = [largest] + [least] * (number_of - 1), total - largest - least * (number_of - 1)
    while rest > 0:
        candidates = [i for i in range(1, number_of) if counts[i] < largest] or [i for i in range(1, number_of) if counts[i] < reach]
        mass, remaining = sum([weights[i] for i in candidates]), rest
        for i in candidates:
            addition = min(reach - counts[i], max(1, remaining * weights[i] // mass), rest)
            counts[i] = counts[i] + addition
            rest = rest - addition
    return np.array(counts)


def bell_draw(key, dims, width, reach, shards=(), held_as=jnp.bfloat16):
    gain = shard_levels(key, dims, shards, -0.22, 0.18) if shards else 1.0
    array = jax.random.normal(key, dims, jnp.float32) * width * gain
    return jnp.minimum(jnp.maximum(array, -reach), reach).astype(held_as)


def setup_inputs(seed: int = 0) -> dict:
    key_list = jax.random.split(jax.random.key(seed), 10)
    source_field = bell_draw(key_list[0], (2, NRHS, PANELS), 1.0, 6.0, ((1, 2), (2, 128)), jnp.float32)
    near_blocks = bell_draw(key_list[1], (CLUSTERS, NEAR, 2, LEAF, LEAF), (2 * NEAR * LEAF) ** -0.5, 0.125, ((0, 128),))
    near_offsets = draw_near_offsets(jax.random.fold_in(key_list[9], 71), 0)
    far_v = bell_draw(key_list[3], (FAR_TOTAL, 2, RANK, LEAF), (2 * LEAF) ** -0.5, 0.25, ((0, 128),))
    far_u = bell_draw(key_list[4], (FAR_TOTAL, 2, RANK, LEAF), (4 * RANK * FAR_DEV // CL_DEV) ** -0.5, 0.109375, ((0, 128), (3, 2)))
    far_rank = plant(jax.random.randint(key_list[5], (FAR_TOTAL,), RANK // 3, RANK + 1), jax.random.fold_in(key_list[5], 1), RANK // 3, RANK).astype(jnp.int32)
    far_col_local = plant(jax.random.randint(key_list[6], (FAR_TOTAL,), 0, CL_DEV), jax.random.fold_in(key_list[6], 1), 0, CL_DEV - 1).astype(jnp.int32)
    far_dest_keys = jax.random.split(jax.random.fold_in(key_list[7], 1), FAR_TOTAL // FAR_DEV)
    far_dest_turns = jax.random.permutation(jax.random.fold_in(key_list[7], 3), FAR_TOTAL // FAR_DEV)
    far_dest = jax.vmap(lambda own, number: routed_block(jax.random.fold_in(key_list[7], 2), own, number, FAR_DEV, N_ROW, 1, CAP, 2))(far_dest_keys, far_dest_turns).reshape((FAR_TOTAL, 1))
    far_row_local = plant(jax.random.randint(key_list[8], (FAR_TOTAL,), 0, CL_DEV), jax.random.fold_in(key_list[8], 1), 0, CL_DEV - 1).astype(jnp.int32)
    return dict(source_field=source_field, near_blocks=near_blocks, near_offsets=near_offsets, far_v=far_v, far_u=far_u, far_rank=far_rank, far_col_local=far_col_local, far_dest=far_dest, far_row_local=far_row_local)


def near_apply(padded, near_blocks, centres):
    blocks_grouped = near_blocks.reshape(N_ROW, CL_DEV, NEAR, 2, LEAF, LEAF)
    centres_grouped = centres.reshape(N_ROW, CL_DEV, NEAR)

    def per_group(inputs):
        blocks, centre_ids = inputs
        columns = padded[:, :, centre_ids, :]
        products = jnp.einsum("ikapl,crikl->acrip", blocks.astype(jnp.float32), columns.astype(jnp.float32))
        real_part = products[0, 0] - products[1, 1]
        imag_part = products[0, 1] + products[1, 0]
        return jnp.stack([real_part, imag_part])

    grouped = lax.map(per_group, (blocks_grouped, centres_grouped))
    return jnp.moveaxis(grouped, 0, 2).reshape(2, NRHS, CLUSTERS, LEAF)


def far_apply(clusters_view, far_v, far_u, col_cluster, row_cluster, keep_mask):
    v_grouped = far_v.reshape(N_ROW, FAR_DEV, 2, RANK, LEAF)
    u_grouped = far_u.reshape(N_ROW, FAR_DEV, 2, RANK, LEAF)
    col_grouped = col_cluster.reshape(N_ROW, FAR_DEV)
    row_grouped = row_cluster.reshape(N_ROW, FAR_DEV)
    keep_grouped = keep_mask.reshape(N_ROW, FAR_DEV, RANK, 1)

    def per_group(total_far, inputs):
        v_blocks, u_blocks, col_ids, row_ids, kept = inputs
        picked = clusters_view[:, :, col_ids, :]
        inner = jnp.einsum("bakl,crbl->acbkr", v_blocks.astype(jnp.float32), picked.astype(jnp.float32))
        coef_real = jnp.where(kept, inner[0, 0] - inner[1, 1], 0.0)
        coef_imag = jnp.where(kept, inner[0, 1] + inner[1, 0], 0.0)
        coefs = jnp.stack([coef_real, coef_imag]).astype(jnp.bfloat16).astype(jnp.float32)
        expanded = jnp.einsum("bakl,cbkr->acrbl", u_blocks.astype(jnp.float32), coefs)
        contrib = jnp.stack([expanded[0, 0] - expanded[1, 1], expanded[0, 1] + expanded[1, 0]])
        total_far = total_far.at[:, :, row_ids, :].add(contrib)
        return total_far, None

    start = jnp.zeros((2, NRHS, CLUSTERS, LEAF), jnp.float32)
    total_far, unused = lax.scan(per_group, start, (v_grouped, u_grouped, col_grouped, row_grouped, keep_grouped))
    return total_far


def reference(source_field, near_blocks, near_offsets, far_v, far_u, far_rank, far_col_local, far_dest, far_row_local):
    owner_dev = jnp.arange(FAR_TOTAL, dtype=jnp.int32) // FAR_DEV
    col_cluster = (owner_dev * CL_DEV + far_col_local).astype(jnp.int32)
    row_cluster = (far_dest[:, 0] * CL_DEV + far_row_local).astype(jnp.int32)
    keep_mask = jnp.arange(RANK, dtype=jnp.int32)[None, :] < far_rank[:, None]
    centres = (jnp.arange(CLUSTERS, dtype=jnp.int32)[:, None] + near_offsets + WIN).astype(jnp.int32)
    current = source_field
    for application in range(APPS):
        rounded = current.astype(jnp.bfloat16)
        clusters_view = rounded.reshape(2, NRHS, CLUSTERS, LEAF)
        padded = jnp.pad(clusters_view, ((0, 0), (0, 0), (WIN, WIN), (0, 0)))
        near_term = near_apply(padded, near_blocks, centres)
        far_term = far_apply(clusters_view, far_v, far_u, col_cluster, row_cluster, keep_mask)
        current = (near_term + far_term).reshape(2, NRHS, PANELS)
    return current
```

```python
import functools

import jax
import jax.numpy as jnp
from jax import lax
from jax.experimental import pallas as pl
from jax.experimental.pallas import tpu as pltpu
from jax.sharding import PartitionSpec as P

APPS = 4
BF = jnp.bfloat16
F32 = jnp.float32
VMEM_LIMIT = 56 * 1024 * 1024


def dot(a, b):
    return jnp.dot(a, b, preferred_element_type=F32)


def next_slot(count_ref, destination):
    slot = count_ref[destination]
    count_ref[destination] = slot + 1
    return slot


def clear_counts(count_ref, count):
    def body(i, carry):
        count_ref[i] = 0
        return carry

    lax.fori_loop(0, count, body, 0)


def place_u_kernel(dest_ref, u_ref, out_ref, count_ref):
    clear_counts(count_ref, out_ref.shape[0])
    out_ref[...] = jnp.zeros_like(out_ref)
    half = u_ref.shape[3]

    def body(b, carry):
        d = dest_ref[b]
        s = next_slot(count_ref, d)
        for c in range(2):
            lane = pl.multiple_of(s * (2 * half) + c * half, half)
            out_ref[d, :, pl.ds(lane, half)] = u_ref[b, c]
        return carry

    lax.fori_loop(0, u_ref.shape[0], body, 0)


def place_v_kernel(
    dest_ref, rank_ref, col_ref, row_ref, v_ref, out_ref, mask_ref, tag_ref, count_ref
):
    clear_counts(count_ref, out_ref.shape[0])
    out_ref[...] = jnp.zeros_like(out_ref)
    mask_ref[...] = jnp.zeros_like(mask_ref)
    tag_ref[...] = jnp.zeros_like(tag_ref)
    rank_size, leaf = v_ref.shape[2], v_ref.shape[3]
    group = lax.broadcasted_iota(jnp.int32, (rank_size, 256), 1) // 64
    index = lax.broadcasted_iota(jnp.int32, (rank_size, 256), 0)
    lane = lax.broadcasted_iota(jnp.int32, (rank_size, 128), 1)

    def body(b, carry):
        d = dest_ref[b]
        s = next_slot(count_ref, d)
        for c in range(2):
            at = pl.multiple_of(s * (2 * leaf) + c * leaf, leaf)
            out_ref[d, :, pl.ds(at, leaf)] = v_ref[b, c]
        kept = (group == col_ref[b]) & (index < rank_ref[b])
        mask_ref[d, :, pl.ds(pl.multiple_of(s * 256, 256), 256)] = jnp.where(kept, 1.0, 0.0).astype(
            BF
        )
        tag = jnp.where(lane == s * 64 + 48 + row_ref[b], 1.0, 0.0)
        tag_ref[d] = (tag_ref[d].astype(F32) + tag).astype(BF)
        return carry

    lax.fori_loop(0, v_ref.shape[0], body, 0)


def near_kernel(offset_ref, left_ref, low_ref, high_ref, right_ref, a_ref, out_ref, xa_ref, xb_ref):
    i = pl.program_id(0)

    @pl.when(i == 0)
    def _():
        pad = jnp.zeros((16, 256), F32)
        for q, ref in enumerate((left_ref, low_ref, high_ref, right_ref)):
            for j in range(2):
                x = ref[j].astype(F32)
                re, im = x[:24], x[24:]
                xa_ref[q * 2 + j] = jnp.concatenate([re, im, pad], axis=0).T.astype(BF)
                xb_ref[q * 2 + j] = jnp.concatenate([-im, re, pad], axis=0).T.astype(BF)

    total = jnp.zeros((256, 64), F32)
    for k in range(a_ref.shape[1]):
        at = i + offset_ref[i, k] + 2
        total += dot(a_ref[0, k, 0], xa_ref[at]) + dot(a_ref[0, k, 1], xb_ref[at])
    out_ref[...] = total.T[:48]


def stage_kernel(do_u, do_v, steps_u, *refs):
    refs = list(refs)
    core_ref = refs.pop(0)
    i = pl.program_id(0)
    if do_u:
        c_ref, own_ref, other_ref, near_ref = refs[:4]
        refs = refs[4:]
    else:
        field_ref = refs.pop(0)
    if do_v:
        v_ref, mask_ref, tag_ref = refs[:3]
        refs = refs[3:]
        message_ref, low_ref, high_ref = refs[:3]
        refs = refs[3:]
    else:
        out_ref = refs.pop(0)
    if do_u:
        total_ref = refs.pop(0)
    if do_v:
        xw_ref, fold_ref = refs

    def prepare(clusters):
        pad = jnp.zeros((16, 256), F32)
        first, second = [], []
        for m, x in enumerate(clusters):
            rounded = x.astype(BF)
            (low_ref if m < 2 else high_ref)[m % 2] = rounded
            wide = rounded.astype(F32)
            re, im = wide[:24], wide[24:]
            first += [re, im, pad]
            second += [-im, re, pad]
        xw_ref[0] = jnp.concatenate(first, axis=0).T.astype(BF)
        xw_ref[1] = jnp.concatenate(second, axis=0).T.astype(BF)
        row = lax.broadcasted_iota(jnp.int32, (512, 128), 0)
        lane = lax.broadcasted_iota(jnp.int32, (512, 128), 1)
        same = (row // 256 == lane // 64) & (row % 64 == lane % 64)
        fold_ref[...] = jnp.where(same, 1.0, 0.0).astype(BF)

    if do_u:

        @pl.when(i == 0)
        def _():
            total_ref[...] = jnp.zeros_like(total_ref)

        @pl.when(i < steps_u)
        def _():
            turned = c_ref[...].astype(F32).T
            for s in range(2):
                base = turned[s * 64 : s * 64 + 48]
                weights = jnp.concatenate(
                    [
                        (base * turned[s * 64 + 48 + o : s * 64 + 49 + o]).astype(BF)
                        for o in range(4)
                    ],
                    axis=0,
                )
                lanes = slice(s * 256, s * 256 + 256)
                total_ref[0] += dot(weights, own_ref[:, lanes])
                total_ref[1] += dot(weights, other_ref[:, lanes])

        @pl.when(i == steps_u - 1)
        def _():
            first_core = core_ref[0] == 0
            clusters = []
            for o in range(4):
                halves = []
                for w in range(2):
                    z = total_ref[w, o * 48 : o * 48 + 48]
                    re = z[:24, :128] - z[24:, 128:]
                    im = z[24:, :128] + z[:24, 128:]
                    halves.append(jnp.concatenate([re, im], axis=0))
                x = jnp.concatenate(
                    [
                        jnp.where(first_core, halves[0], halves[1]),
                        jnp.where(first_core, halves[1], halves[0]),
                    ],
                    axis=1,
                )
                clusters.append(x + near_ref[:, o * 256 : o * 256 + 256])
            if do_v:
                prepare(clusters)
            else:
                for o in range(4):
                    out_ref[:, o * 256 : o * 256 + 256] = clusters[o]
    else:

        @pl.when(i == 0)
        def _():
            prepare([field_ref[:, m * 256 : m * 256 + 256] for m in range(4)])

    if do_v:

        @pl.when(i >= steps_u)
        def _():
            picked = []
            for s in range(2):
                base = s * 512
                p = dot(v_ref[:, base : base + 256], xw_ref[0])
                p += dot(v_ref[:, base + 256 : base + 512], xw_ref[1])
                picked.append(p.astype(BF) * mask_ref[:, s * 256 : s * 256 + 256])
            folded = dot(jnp.concatenate(picked, axis=1), fold_ref[...])
            message_ref[...] = (folded + tag_ref[...].astype(F32)).astype(BF)


def stage(do_u, do_v, core, *operands):
    steps = 4
    steps_u = steps if do_u else 0
    total_rows = operands[0].shape[0] if do_u else operands[1].shape[0]
    rows = total_rows // steps
    grid = steps_u + (steps if do_v else 0)

    def in_u(i, core_ref):
        return (jnp.minimum(i, steps - 1), 0)

    def in_v(i, core_ref):
        return (jnp.maximum(i - steps_u, 0), 0)

    def whole(rank):
        return lambda i, core_ref: (0,) * rank

    in_specs, scratch = [], []
    if do_u:
        in_specs += [
            pl.BlockSpec((rows, 128), in_u),
            pl.BlockSpec((rows, 512), in_u),
            pl.BlockSpec((rows, 512), in_u),
            pl.BlockSpec((48, 1024), whole(2)),
        ]
        scratch.append(pltpu.VMEM((2, 192, 256), F32))
    else:
        in_specs.append(pl.BlockSpec((48, 1024), whole(2)))
    if do_v:
        in_specs += [
            pl.BlockSpec((rows, 1024), in_v),
            pl.BlockSpec((rows, 512), in_v),
            pl.BlockSpec((rows, 128), in_v),
        ]
        out_shape = [
            jax.ShapeDtypeStruct((total_rows, 128), BF),
            jax.ShapeDtypeStruct((2, 48, 256), BF),
            jax.ShapeDtypeStruct((2, 48, 256), BF),
        ]
        out_specs = [
            pl.BlockSpec((rows, 128), in_v),
            pl.BlockSpec((2, 48, 256), whole(3)),
            pl.BlockSpec((2, 48, 256), whole(3)),
        ]
        scratch += [pltpu.VMEM((2, 256, 256), BF), pltpu.VMEM((512, 128), BF)]
    else:
        out_shape = jax.ShapeDtypeStruct((48, 1024), F32)
        out_specs = pl.BlockSpec((48, 1024), whole(2))
    return pl.pallas_call(
        functools.partial(stage_kernel, do_u, do_v, steps_u),
        grid_spec=pltpu.PrefetchScalarGridSpec(
            num_scalar_prefetch=1,
            grid=(grid,),
            in_specs=in_specs,
            out_specs=out_specs,
            scratch_shapes=scratch,
        ),
        out_shape=out_shape,
        compiler_params=pltpu.CompilerParams(vmem_limit_bytes=VMEM_LIMIT),
        cost_estimate=pl.CostEstimate(
            flops=6_000_000_000, bytes_accessed=16_000_000, transcendentals=0
        ),
    )(core, *operands)


def near_call(offsets, left, low, high, right, blocks):
    clusters, near = blocks.shape[:2]
    whole = pl.BlockSpec((2, 48, 256), lambda i, offset_ref: (0, 0, 0))
    return pl.pallas_call(
        near_kernel,
        grid_spec=pltpu.PrefetchScalarGridSpec(
            num_scalar_prefetch=1,
            grid=(clusters,),
            in_specs=[whole] * 4
            + [pl.BlockSpec((1, near, 2, 256, 256), lambda i, offset_ref: (i, 0, 0, 0, 0))],
            out_specs=pl.BlockSpec((48, 256), lambda i, offset_ref: (0, i)),
            scratch_shapes=[pltpu.VMEM((8, 256, 64), BF), pltpu.VMEM((8, 256, 64), BF)],
        ),
        out_shape=jax.ShapeDtypeStruct((48, clusters * 256), F32),
        compiler_params=pltpu.CompilerParams(vmem_limit_bytes=VMEM_LIMIT),
        cost_estimate=pl.CostEstimate(
            flops=3_000_000_000, bytes_accessed=4_500_000, transcendentals=0
        ),
    )(offsets, left, low, high, right, blocks)


def place_u(dest, far_u, count):
    return pl.pallas_call(
        place_u_kernel,
        in_specs=[
            pl.BlockSpec(memory_space=pltpu.SMEM),
            pl.BlockSpec(memory_space=pltpu.VMEM),
        ],
        out_specs=pl.BlockSpec(memory_space=pltpu.VMEM),
        out_shape=jax.ShapeDtypeStruct((count, far_u.shape[2], 4 * far_u.shape[3]), BF),
        scratch_shapes=[pltpu.SMEM((count,), jnp.int32)],
        compiler_params=pltpu.CompilerParams(vmem_limit_bytes=VMEM_LIMIT),
    )(dest, far_u)


def place_v(dest, rank, col, row, far_v, count):
    rank_size, leaf = far_v.shape[2:]
    return pl.pallas_call(
        place_v_kernel,
        in_specs=[pl.BlockSpec(memory_space=pltpu.SMEM)] * 4
        + [pl.BlockSpec(memory_space=pltpu.VMEM)],
        out_specs=[pl.BlockSpec(memory_space=pltpu.VMEM)] * 3,
        out_shape=[
            jax.ShapeDtypeStruct((count, rank_size, 4 * leaf), BF),
            jax.ShapeDtypeStruct((count, rank_size, 512), BF),
            jax.ShapeDtypeStruct((count, rank_size, 128), BF),
        ],
        scratch_shapes=[pltpu.SMEM((count,), jnp.int32)],
        compiler_params=pltpu.CompilerParams(vmem_limit_bytes=VMEM_LIMIT),
        cost_estimate=pl.CostEstimate(
            flops=6_000_000_000, bytes_accessed=16_000_000, transcendentals=0
        ),
    )(dest, rank, col, row, far_v)


def on_device(
    source_field,
    near_blocks,
    near_offsets,
    far_v,
    far_u,
    far_rank,
    far_col_local,
    far_dest,
    far_row_local,
):
    parts, rhs_dev, panels_dev = source_field.shape
    rank_size = far_v.shape[2]
    count = lax.axis_size("row")
    forward = [(i, i + 1) for i in range(count - 1)]
    backward = [(i + 1, i) for i in range(count - 1)]
    core = lax.axis_index("rhs").astype(jnp.int32).reshape(1)
    dest = far_dest.reshape(-1)

    def exchange(x):
        return lax.all_to_all(x, "row", split_axis=0, concat_axis=0, tiled=True)

    u_own = exchange(place_u(dest, far_u, count)).reshape(count * rank_size, -1)
    u_other = lax.ppermute(u_own, "rhs", [(0, 1), (1, 0)])
    v_slots, mask, tag = place_v(dest, far_rank, far_col_local, far_row_local, far_v, count)
    v_slots = v_slots.reshape(count * rank_size, -1)
    mask = mask.reshape(count * rank_size, -1)
    tag = tag.reshape(count * rank_size, -1)
    message, low, high = stage(
        False, True, core, source_field.reshape(parts * rhs_dev, panels_dev), v_slots, mask, tag
    )
    for application in range(APPS):
        left = lax.ppermute(high, "row", forward)
        right = lax.ppermute(low, "row", backward)
        arrived = exchange(message.reshape(count, rank_size, 128)).reshape(-1, 128)
        near_term = near_call(near_offsets, left, low, high, right, near_blocks)
        if application < APPS - 1:
            message, low, high = stage(
                True, True, core, arrived, u_own, u_other, near_term, v_slots, mask, tag
            )
    result = stage(True, False, core, arrived, u_own, u_other, near_term)
    return result.reshape(parts, rhs_dev, panels_dev)


def solution(mesh):
    return jax.shard_map(
        on_device,
        mesh=mesh,
        in_specs=(
            P(None, "rhs", "row"),
            P("row", None, None, None, None),
            P("row", None),
            P("row", None, None, None),
            P("row", None, None, "rhs"),
            P("row"),
            P("row"),
            P("row", None),
            P("row"),
        ),
        out_specs=P(None, "rhs", "row"),
        check_vma=False,
    )
```

```python
import functools

import jax
import jax.numpy as jnp
from jax import lax
from jax.experimental import pallas as pl
from jax.experimental.pallas import tpu as pltpu
from jax.sharding import PartitionSpec as P

APPS = 4
BF = jnp.bfloat16
F32 = jnp.float32
VMEM_LIMIT = 20 * 1024 * 1024


def dot(a, b):
    return jnp.dot(a, b, preferred_element_type=F32)


def next_slot(count_ref, destination):
    slot = count_ref[destination]
    count_ref[destination] = slot + 1
    return slot


def clear_counts(count_ref, count):
    def body(i, carry):
        count_ref[i] = 0
        return carry

    lax.fori_loop(0, count, body, 0)


def place_u_kernel(dest_ref, u_ref, out_ref, count_ref):
    clear_counts(count_ref, out_ref.shape[0])
    out_ref[...] = jnp.zeros_like(out_ref)
    half = u_ref.shape[3]

    def body(b, carry):
        d = dest_ref[b]
        s = next_slot(count_ref, d)
        for c in range(2):
            lane = pl.multiple_of(s * (2 * half) + c * half, half)
            out_ref[d, :, pl.ds(lane, half)] = u_ref[b, c]
        return carry

    lax.fori_loop(0, u_ref.shape[0], body, 0)


def place_v_kernel(
    dest_ref, rank_ref, col_ref, row_ref, v_ref, out_ref, mask_ref, tag_ref, count_ref
):
    clear_counts(count_ref, out_ref.shape[0])
    out_ref[...] = jnp.zeros_like(out_ref)
    mask_ref[...] = jnp.zeros_like(mask_ref)
    tag_ref[...] = jnp.zeros_like(tag_ref)
    rank_size, leaf = v_ref.shape[2], v_ref.shape[3]
    group = lax.broadcasted_iota(jnp.int32, (rank_size, 256), 1) // 64
    index = lax.broadcasted_iota(jnp.int32, (rank_size, 256), 0)
    lane = lax.broadcasted_iota(jnp.int32, (rank_size, 128), 1)

    def body(b, carry):
        d = dest_ref[b]
        s = next_slot(count_ref, d)
        for c in range(2):
            at = pl.multiple_of(s * (2 * leaf) + c * leaf, leaf)
            out_ref[d, :, pl.ds(at, leaf)] = v_ref[b, c]
        kept = (group == col_ref[b]) & (index < rank_ref[b])
        mask_ref[d, :, pl.ds(pl.multiple_of(s * 256, 256), 256)] = jnp.where(kept, 1.0, 0.0).astype(
            BF
        )
        tag = jnp.where(lane == s * 64 + 48 + row_ref[b], 1.0, 0.0)
        tag_ref[d] = (tag_ref[d].astype(F32) + tag).astype(BF)
        return carry

    lax.fori_loop(0, v_ref.shape[0], body, 0)


def near_kernel(offset_ref, left_ref, low_ref, high_ref, right_ref, a_ref, out_ref, xa_ref, xb_ref):
    pad = jnp.zeros((16, 256), F32)
    for q, ref in enumerate((left_ref, low_ref, high_ref, right_ref)):
        for j in range(2):
            x = ref[j].astype(F32)
            re, im = x[:24], x[24:]
            xa_ref[q * 2 + j] = jnp.concatenate([re, im, pad], axis=0).T.astype(BF)
            xb_ref[q * 2 + j] = jnp.concatenate([-im, re, pad], axis=0).T.astype(BF)
    for i in range(a_ref.shape[0]):
        total = jnp.zeros((256, 64), F32)
        for k in range(a_ref.shape[1]):
            at = i + offset_ref[i, k] + 2
            total += dot(a_ref[i, k, 0], xa_ref[at]) + dot(a_ref[i, k, 1], xb_ref[at])
        out_ref[:, i * 256 : i * 256 + 256] = total.T[:48]


def stage_kernel(do_u, do_v, steps, *refs):
    refs = list(refs)
    core_ref = refs.pop(0)
    if do_u:
        c_ref, own_ref, other_ref, near_ref = refs[:4]
        refs = refs[4:]
        total_rows = c_ref.shape[0]
    else:
        field_ref = refs.pop(0)
    if do_v:
        v_ref, mask_ref, tag_ref = refs[:3]
        refs = refs[3:]
        total_rows = v_ref.shape[0]
        message_ref, low_ref, high_ref = refs
    else:
        (out_ref,) = refs
    rows = total_rows // steps

    if do_u:
        totals = [jnp.zeros((192, 256), F32) for w in range(2)]
        for step in range(steps):
            at = slice(step * rows, step * rows + rows)
            turned = c_ref[at].astype(F32).T
            for s in range(2):
                base = turned[s * 64 : s * 64 + 48]
                weights = jnp.concatenate(
                    [
                        (base * turned[s * 64 + 48 + o : s * 64 + 49 + o]).astype(BF)
                        for o in range(4)
                    ],
                    axis=0,
                )
                lanes = slice(s * 256, s * 256 + 256)
                totals[0] += dot(weights, own_ref[at, lanes])
                totals[1] += dot(weights, other_ref[at, lanes])
        first_core = core_ref[0] == 0
        clusters = []
        for o in range(4):
            halves = []
            for w in range(2):
                z = totals[w][o * 48 : o * 48 + 48]
                re = z[:24, :128] - z[24:, 128:]
                im = z[24:, :128] + z[:24, 128:]
                halves.append(jnp.concatenate([re, im], axis=0))
            x = jnp.concatenate(
                [
                    jnp.where(first_core, halves[0], halves[1]),
                    jnp.where(first_core, halves[1], halves[0]),
                ],
                axis=1,
            )
            clusters.append(x + near_ref[:, o * 256 : o * 256 + 256])
    else:
        clusters = [field_ref[:, m * 256 : m * 256 + 256] for m in range(4)]

    if not do_v:
        for o in range(4):
            out_ref[:, o * 256 : o * 256 + 256] = clusters[o]
        return

    pad = jnp.zeros((16, 256), F32)
    first, second = [], []
    for m, x in enumerate(clusters):
        rounded = x.astype(BF)
        (low_ref if m < 2 else high_ref)[m % 2] = rounded
        wide = rounded.astype(F32)
        re, im = wide[:24], wide[24:]
        first += [re, im, pad]
        second += [-im, re, pad]
    columns = jnp.concatenate(
        [
            jnp.concatenate(first, axis=0).T.astype(BF),
            jnp.concatenate(second, axis=0).T.astype(BF),
        ],
        axis=0,
    )
    row = lax.broadcasted_iota(jnp.int32, (512, 128), 0)
    lane = lax.broadcasted_iota(jnp.int32, (512, 128), 1)
    same = (row // 256 == lane // 64) & (row % 64 == lane % 64)
    fold = jnp.where(same, 1.0, 0.0).astype(BF)
    for step in range(steps):
        at = slice(step * rows, step * rows + rows)
        picked = []
        for s in range(2):
            p = dot(v_ref[at, s * 512 : s * 512 + 512], columns)
            picked.append(p.astype(BF) * mask_ref[at, s * 256 : s * 256 + 256])
        folded = dot(jnp.concatenate(picked, axis=1), fold)
        message_ref[at] = (folded + tag_ref[at].astype(F32)).astype(BF)


def whole_vmem(count):
    return [pl.BlockSpec(memory_space=pltpu.VMEM)] * count


SCALARS = pl.BlockSpec(memory_space=pltpu.SMEM)


def stage(do_u, do_v, core, *operands):
    if do_v:
        total_rows = operands[-1].shape[0]
        out_shape = [
            jax.ShapeDtypeStruct((total_rows, 128), BF),
            jax.ShapeDtypeStruct((2, 48, 256), BF),
            jax.ShapeDtypeStruct((2, 48, 256), BF),
        ]
        out_specs = whole_vmem(3)
    else:
        out_shape = jax.ShapeDtypeStruct((48, 1024), F32)
        out_specs = whole_vmem(1)[0]
    return pl.pallas_call(
        functools.partial(stage_kernel, do_u, do_v, 4),
        in_specs=[SCALARS] + whole_vmem(len(operands)),
        out_specs=out_specs,
        out_shape=out_shape,
        compiler_params=pltpu.CompilerParams(vmem_limit_bytes=VMEM_LIMIT),
        cost_estimate=pl.CostEstimate(
            flops=4_000_000_000, bytes_accessed=1_000_000, transcendentals=0
        ),
    )(core, *operands)


def near_call(offsets, left, low, high, right, blocks):
    return pl.pallas_call(
        near_kernel,
        in_specs=[SCALARS] + whole_vmem(5),
        out_specs=whole_vmem(1)[0],
        out_shape=jax.ShapeDtypeStruct((48, blocks.shape[0] * 256), F32),
        scratch_shapes=[pltpu.VMEM((8, 256, 64), BF), pltpu.VMEM((8, 256, 64), BF)],
        compiler_params=pltpu.CompilerParams(vmem_limit_bytes=VMEM_LIMIT),
        cost_estimate=pl.CostEstimate(
            flops=3_000_000_000, bytes_accessed=1_000_000, transcendentals=0
        ),
    )(offsets, left, low, high, right, blocks)


def place_u(dest, far_u, count):
    return pl.pallas_call(
        place_u_kernel,
        in_specs=[
            pl.BlockSpec(memory_space=pltpu.SMEM),
            pl.BlockSpec(memory_space=pltpu.VMEM),
        ],
        out_specs=pl.BlockSpec(memory_space=pltpu.VMEM),
        out_shape=jax.ShapeDtypeStruct((count, far_u.shape[2], 4 * far_u.shape[3]), BF),
        scratch_shapes=[pltpu.SMEM((count,), jnp.int32)],
        compiler_params=pltpu.CompilerParams(vmem_limit_bytes=VMEM_LIMIT),
    )(dest, far_u)


def place_v(dest, rank, col, row, far_v, count):
    rank_size, leaf = far_v.shape[2:]
    return pl.pallas_call(
        place_v_kernel,
        in_specs=[pl.BlockSpec(memory_space=pltpu.SMEM)] * 4
        + [pl.BlockSpec(memory_space=pltpu.VMEM)],
        out_specs=[pl.BlockSpec(memory_space=pltpu.VMEM)] * 3,
        out_shape=[
            jax.ShapeDtypeStruct((count, rank_size, 4 * leaf), BF),
            jax.ShapeDtypeStruct((count, rank_size, 512), BF),
            jax.ShapeDtypeStruct((count, rank_size, 128), BF),
        ],
        scratch_shapes=[pltpu.SMEM((count,), jnp.int32)],
        compiler_params=pltpu.CompilerParams(vmem_limit_bytes=VMEM_LIMIT),
        cost_estimate=pl.CostEstimate(
            flops=6_000_000_000, bytes_accessed=16_000_000, transcendentals=0
        ),
    )(dest, rank, col, row, far_v)


def on_device(
    source_field,
    near_blocks,
    near_offsets,
    far_v,
    far_u,
    far_rank,
    far_col_local,
    far_dest,
    far_row_local,
):
    parts, rhs_dev, panels_dev = source_field.shape
    rank_size = far_v.shape[2]
    count = lax.axis_size("row")
    forward = [(i, i + 1) for i in range(count - 1)]
    backward = [(i + 1, i) for i in range(count - 1)]
    core = lax.axis_index("rhs").astype(jnp.int32).reshape(1)
    dest = far_dest.reshape(-1)

    def exchange(x):
        return lax.all_to_all(x, "row", split_axis=0, concat_axis=0, tiled=True)

    u_own = exchange(place_u(dest, far_u, count))
    v_slots, mask, tag = place_v(dest, far_rank, far_col_local, far_row_local, far_v, count)
    v_slots = v_slots.reshape(count * rank_size, -1)
    mask = mask.reshape(count * rank_size, -1)
    tag = tag.reshape(count * rank_size, -1)
    message, low, high = stage(
        False, True, core, source_field.reshape(parts * rhs_dev, panels_dev), v_slots, mask, tag
    )
    for application in range(APPS):
        left = lax.ppermute(high, "row", forward)
        right = lax.ppermute(low, "row", backward)
        near_term = near_call(near_offsets, left, low, high, right, near_blocks)
        if application == 0:
            u_own, message = lax.optimization_barrier((u_own, message))
            u_own = u_own.reshape(count * rank_size, -1)
            u_other = lax.ppermute(u_own, "rhs", [(0, 1), (1, 0)])
        arrived = exchange(message.reshape(count, rank_size, 128)).reshape(-1, 128)
        if application < APPS - 1:
            message, low, high = stage(
                True, True, core, arrived, u_own, u_other, near_term, v_slots, mask, tag
            )
    result = stage(True, False, core, arrived, u_own, u_other, near_term)
    return result.reshape(parts, rhs_dev, panels_dev)


def solution(mesh):
    return jax.shard_map(
        on_device,
        mesh=mesh,
        in_specs=(
            P(None, "rhs", "row"),
            P("row", None, None, None, None),
            P("row", None),
            P("row", None, None, None),
            P("row", None, None, "rhs"),
            P("row"),
            P("row"),
            P("row", None),
            P("row"),
        ),
        out_specs=P(None, "rhs", "row"),
        check_vma=False,
    )
```

```python
import functools

import jax
import jax.numpy as jnp
from jax import lax
from jax.experimental import pallas as pl
from jax.experimental.pallas import tpu as pltpu
from jax.sharding import PartitionSpec as P

APPS = 4
BF = jnp.bfloat16
F32 = jnp.float32
SETUP_LIMIT = 60 * 1024 * 1024
STAGE_LIMIT = 50 * 1024 * 1024
STEPS = 4
RANK = 24


def dot(a, b):
    return jnp.dot(a, b, preferred_element_type=F32)


def next_slot(count_ref, destination):
    slot = count_ref[destination]
    count_ref[destination] = slot + 1
    return slot


def clear_counts(count_ref, count):
    def body(i, carry):
        count_ref[i] = 0
        return carry

    lax.fori_loop(0, count, body, 0)


def place_u_kernel(dest_ref, u_hbm, out_ref, u_ref, count_ref, sem_ref):
    arrival = pltpu.make_async_copy(u_hbm, u_ref, sem_ref)
    arrival.start()
    clear_counts(count_ref, out_ref.shape[0])
    out_ref[...] = jnp.zeros_like(out_ref)
    half = u_ref.shape[3]
    arrival.wait()

    def body(b, carry):
        d = dest_ref[b]
        s = next_slot(count_ref, d)
        for c in range(2):
            lane = pl.multiple_of(s * (2 * half) + c * half, half)
            out_ref[d, :, pl.ds(lane, half)] = u_ref[b, c]
        return carry

    lax.fori_loop(0, u_ref.shape[0], body, 0, unroll=8)


def stage_kernel(do_u, do_v, steps, *refs):
    refs = list(refs)
    sem_ref = refs.pop()
    core_ref, meta_ref, offset_ref = refs[:3]
    refs = refs[3:]
    if do_u:
        reach_refs, near_hbm, u_hbm, refs = refs[:4], refs[4], refs[5:8], refs[8:]
        total_rows = u_hbm[0].shape[0]
    else:
        field_ref = refs.pop(0)
    if do_v:
        v_hbm = refs.pop(0)
        total_rows = v_hbm.shape[0]
        message_ref, low_ref, high_ref = refs[:3]
        refs = refs[3:]
    else:
        out_ref = refs.pop(0)
    rows = total_rows // steps
    started = []

    def fetch(sources, targets, pieces, size):
        arrivals = []
        for piece in range(pieces):
            at = pl.ds(piece * size, size)
            copies = []
            for source, target in zip(sources, targets):
                copy = pltpu.make_async_copy(
                    source.at[at], target.at[at], sem_ref.at[len(started)]
                )
                copy.start()
                started.append(copy)
                copies.append(copy)
            arrivals.append(copies)
        return arrivals

    if do_u:
        near_ref, u_buffers, xa_ref, xb_ref = refs[0], refs[1:4], refs[4], refs[5]
        refs = refs[6:]
        clusters_dev = near_ref.shape[0]
        near_arrivals = fetch([near_hbm], [near_ref], clusters_dev, 1)
        u_arrivals = fetch(u_hbm, u_buffers, steps, rows)
        c_ref, own_ref, other_ref = u_buffers
    if do_v:
        v_ref, product_ref, sum_ref = refs
        v_arrivals = fetch([v_hbm], [v_ref], steps, rows)
        sum_ref[...] = jnp.zeros_like(sum_ref)

    pad = jnp.zeros((16, 256), F32)
    if do_u:
        for q, ref in enumerate(reach_refs):
            for j in range(2):
                x = ref[j].astype(F32)
                re, im = x[:24], x[24:]
                xa_ref[q * 2 + j] = jnp.concatenate([re, im, pad], axis=0).T.astype(BF)
                xb_ref[q * 2 + j] = jnp.concatenate([-im, re, pad], axis=0).T.astype(BF)
        near_terms = []
        for i in range(clusters_dev):
            near_arrivals[i][0].wait()
            total = jnp.zeros((256, 64), F32)
            for k in range(near_ref.shape[1]):
                at = i + offset_ref[i, k] + 2
                total += dot(near_ref[i, k, 0], xa_ref[at]) + dot(near_ref[i, k, 1], xb_ref[at])
            near_terms.append(total.T[:48])
        totals = [jnp.zeros((192, 256), F32) for w in range(2)]
        for step in range(steps):
            for copy in u_arrivals[step]:
                copy.wait()
            at = slice(step * rows, step * rows + rows)
            turned = c_ref[at].astype(F32).T
            for s in range(2):
                base = turned[s * 64 : s * 64 + 48]
                weights = jnp.concatenate(
                    [
                        (base * turned[s * 64 + 48 + o : s * 64 + 49 + o]).astype(BF)
                        for o in range(4)
                    ],
                    axis=0,
                )
                lanes = slice(s * 256, s * 256 + 256)
                totals[0] += dot(weights, own_ref[at, lanes])
                totals[1] += dot(weights, other_ref[at, lanes])
        first_core = core_ref[0] == 0
        clusters = []
        for o in range(4):
            halves = []
            for w in range(2):
                z = totals[w][o * 48 : o * 48 + 48]
                re = z[:24, :128] - z[24:, 128:]
                im = z[24:, :128] + z[:24, 128:]
                halves.append(jnp.concatenate([re, im], axis=0))
            x = jnp.concatenate(
                [
                    jnp.where(first_core, halves[0], halves[1]),
                    jnp.where(first_core, halves[1], halves[0]),
                ],
                axis=1,
            )
            clusters.append(x + near_terms[o])
    else:
        clusters = [field_ref[:, m * 256 : m * 256 + 256] for m in range(4)]

    if not do_v:
        for o in range(4):
            out_ref[:, o * 256 : o * 256 + 256] = clusters[o]
        return

    first, second = [], []
    for m, x in enumerate(clusters):
        rounded = x.astype(BF)
        (low_ref if m < 2 else high_ref)[m % 2] = rounded
        wide = rounded.astype(F32)
        re, im = wide[:24], wide[24:]
        first += [re, im, pad]
        second += [-im, re, pad]
    columns = jnp.concatenate(
        [
            jnp.concatenate(first, axis=0).T.astype(BF),
            jnp.concatenate(second, axis=0).T.astype(BF),
        ],
        axis=0,
    )
    rank_size = sum_ref.shape[1]
    lane = lax.broadcasted_iota(jnp.int32, (rank_size, 128), 1)
    upper = lane // 64

    def place(b, carry):
        at = pl.multiple_of(b * rank_size, 8)
        pair = pl.multiple_of(meta_ref[1, b], 128)
        x = product_ref[pl.ds(at, rank_size), pl.ds(pair, 128)]
        x = jnp.where(meta_ref[2, b] == 1, x, pltpu.roll(x, 64, 1))
        tag = jnp.where(lane == meta_ref[3, b], 1.0, 0.0)
        sum_ref[meta_ref[0, b]] = jnp.where(upper == meta_ref[4, b], x + tag, 0.0)
        return carry

    blocks = rows // rank_size
    for step in range(steps):
        for copy in v_arrivals[step]:
            copy.wait()
        at = slice(step * rows, step * rows + rows)
        product_ref[at] = dot(v_ref[at], columns)
        lax.fori_loop(step * blocks, step * blocks + blocks, place, 0, unroll=16)
    half = sum_ref.shape[0] // 2
    both = sum_ref[:half] + sum_ref[half:]
    message_ref[...] = both.reshape(total_rows, 128).astype(BF)


def whole_vmem(count):
    return [pl.BlockSpec(memory_space=pltpu.VMEM)] * count


SCALARS = pl.BlockSpec(memory_space=pltpu.SMEM)


def stage(do_u, do_v, scalars, local, streamed):
    steps = STEPS
    in_hbm = pl.BlockSpec(memory_space=pl.ANY)
    scratch = [pltpu.VMEM(x.shape, BF) for x in streamed]
    total_rows = streamed[-1].shape[0]
    copies = 0
    if do_u:
        copies += streamed[0].shape[0] + 3 * steps
        scratch[4:4] = [pltpu.VMEM((8, 256, 64), BF), pltpu.VMEM((8, 256, 64), BF)]
    if do_v:
        rank_size = RANK
        out_shape = [
            jax.ShapeDtypeStruct((total_rows, 128), BF),
            jax.ShapeDtypeStruct((2, 48, 256), BF),
            jax.ShapeDtypeStruct((2, 48, 256), BF),
        ]
        out_specs = whole_vmem(3)
        scratch += [
            pltpu.VMEM((total_rows, 256), F32),
            pltpu.VMEM((2 * (total_rows // rank_size), rank_size, 128), F32),
        ]
        copies += steps
    else:
        out_shape = jax.ShapeDtypeStruct((48, 1024), F32)
        out_specs = whole_vmem(1)[0]
    return pl.pallas_call(
        functools.partial(stage_kernel, do_u, do_v, steps),
        in_specs=[SCALARS] * 3 + whole_vmem(len(local)) + [in_hbm] * len(streamed),
        out_specs=out_specs,
        out_shape=out_shape,
        scratch_shapes=scratch + [pltpu.SemaphoreType.DMA((copies,))],
        compiler_params=pltpu.CompilerParams(vmem_limit_bytes=STAGE_LIMIT),
        cost_estimate=pl.CostEstimate(
            flops=4_000_000_000, bytes_accessed=1_000_000, transcendentals=0
        ),
    )(*scalars, *local, *streamed)


def place_u(dest, far_u, count):
    return pl.pallas_call(
        place_u_kernel,
        in_specs=[SCALARS, pl.BlockSpec(memory_space=pl.ANY)],
        out_specs=pl.BlockSpec(memory_space=pltpu.VMEM),
        out_shape=jax.ShapeDtypeStruct((count, far_u.shape[2], 4 * far_u.shape[3]), BF),
        scratch_shapes=[
            pltpu.VMEM(far_u.shape, BF),
            pltpu.SMEM((count,), jnp.int32),
            pltpu.SemaphoreType.DMA,
        ],
        compiler_params=pltpu.CompilerParams(vmem_limit_bytes=SETUP_LIMIT),
    )(dest, far_u)


def on_device(
    source_field,
    near_blocks,
    near_offsets,
    far_v,
    far_u,
    far_rank,
    far_col_local,
    far_dest,
    far_row_local,
):
    parts, rhs_dev, panels_dev = source_field.shape
    rank_size = far_v.shape[2]
    count = lax.axis_size("row")
    forward = [(i, i + 1) for i in range(count - 1)]
    backward = [(i + 1, i) for i in range(count - 1)]
    core = lax.axis_index("rhs").astype(jnp.int32).reshape(1)
    dest = far_dest.reshape(-1)

    def exchange(x):
        return lax.all_to_all(x, "row", split_axis=0, concat_axis=0, tiled=True)

    u_own = exchange(place_u(dest, far_u, count))
    order = jnp.arange(dest.shape[0], dtype=jnp.int32)
    earlier = (dest[None, :] == dest[:, None]) & (order[None, :] < order[:, None])
    slot = jnp.sum(earlier.astype(jnp.int32), axis=1)
    meta = jnp.stack(
        [
            slot * count + dest,
            far_col_local // 2 * 128,
            (far_col_local % 2 == slot).astype(jnp.int32),
            slot * 64 + 48 + far_row_local,
            slot,
        ]
    )
    scalars = [core, meta, near_offsets]
    kept = jnp.arange(rank_size, dtype=jnp.int32)[None, :] < far_rank[:, None]
    v_rows = jnp.where(kept[:, :, None, None], far_v.transpose(0, 2, 1, 3), jnp.zeros((), BF))
    v_rows = v_rows.reshape(dest.shape[0] * rank_size, -1)
    field = source_field.reshape(parts * rhs_dev, panels_dev)
    message, low, high = stage(False, True, scalars, [field], [v_rows])
    for application in range(APPS):
        left = lax.ppermute(high, "row", forward)
        right = lax.ppermute(low, "row", backward)
        if application == 0:
            u_own, message = lax.optimization_barrier((u_own, message))
            u_own = u_own.reshape(count * rank_size, -1)
            u_other = lax.ppermute(u_own, "rhs", [(0, 1), (1, 0)])
        arrived = exchange(message.reshape(count, rank_size, 128)).reshape(-1, 128)
        reach = [left, low, high, right]
        streamed = [near_blocks, arrived, u_own, u_other]
        if application < APPS - 1:
            message, low, high = stage(True, True, scalars, reach, streamed + [v_rows])
    result = stage(True, False, scalars, reach, streamed)
    return result.reshape(parts, rhs_dev, panels_dev)


def solution(mesh):
    return jax.shard_map(
        on_device,
        mesh=mesh,
        in_specs=(
            P(None, "rhs", "row"),
            P("row", None, None, None, None),
            P("row", None),
            P("row", None, None, None),
            P("row", None, None, "rhs"),
            P("row"),
            P("row"),
            P("row", None),
            P("row"),
        ),
        out_specs=P(None, "rhs", "row"),
        check_vma=False,
    )
```

```python
import functools

import jax
import jax.numpy as jnp
from jax import lax
from jax.experimental import pallas as pl
from jax.experimental.pallas import tpu as pltpu
from jax.sharding import PartitionSpec as P

APPS = 4
BF = jnp.bfloat16
F32 = jnp.float32
SETUP_LIMIT = 60 * 1024 * 1024
STAGE_LIMIT = 50 * 1024 * 1024
STEPS = 3
PIECES = 16
RANK = 24


def dot(a, b):
    return jnp.dot(a, b, preferred_element_type=F32)


def next_slot(count_ref, destination):
    slot = count_ref[destination]
    count_ref[destination] = slot + 1
    return slot


def clear_counts(count_ref, count):
    def body(i, carry):
        count_ref[i] = 0
        return carry

    lax.fori_loop(0, count, body, 0)


def place_u_kernel(dest_ref, u_hbm, out_ref, u_ref, count_ref, sem_ref):
    arrival = pltpu.make_async_copy(u_hbm, u_ref, sem_ref)
    arrival.start()
    clear_counts(count_ref, out_ref.shape[0])
    out_ref[...] = jnp.zeros_like(out_ref)
    half = u_ref.shape[3]
    arrival.wait()

    def body(b, carry):
        d = dest_ref[b]
        s = next_slot(count_ref, d)
        for c in range(2):
            lane = pl.multiple_of(s * (2 * half) + c * half, half)
            out_ref[d, :, pl.ds(lane, half)] = u_ref[b, c]
        return carry

    lax.fori_loop(0, u_ref.shape[0], body, 0, unroll=8)


def stage_kernel(do_u, do_v, steps, *refs):
    refs = list(refs)
    sem_ref = refs.pop()
    core_ref, meta_ref, offset_ref = refs[:3]
    refs = refs[3:]
    if do_u:
        reach_refs, near_hbm, u_hbm, refs = refs[:4], refs[4], refs[5:8], refs[8:]
        total_rows = u_hbm[0].shape[0]
    else:
        field_ref = refs.pop(0)
    if do_v:
        v_hbm, tag_ref = refs[:2]
        refs = refs[2:]
        total_rows = v_hbm.shape[0]
        message_ref, low_ref, high_ref = refs[:3]
        refs = refs[3:]
    else:
        out_ref = refs.pop(0)
    rows = total_rows // steps
    started = []

    def fetch(sources, targets, pieces, size):
        arrivals = []
        for piece in range(pieces):
            at = pl.ds(piece * size, size)
            copies = []
            for source, target in zip(sources, targets):
                copy = pltpu.make_async_copy(
                    source.at[at], target.at[at], sem_ref.at[len(started)]
                )
                copy.start()
                started.append(copy)
                copies.append(copy)
            arrivals.append(copies)
        return arrivals

    if do_u:
        near_ref, u_buffers, xa_ref, xb_ref = refs[0], refs[1:4], refs[4], refs[5]
        refs = refs[6:]
        clusters_dev = near_ref.shape[0]
        near_arrivals = fetch([near_hbm], [near_ref], clusters_dev, 1)
        u_arrivals = fetch(u_hbm, u_buffers, steps, rows)
        c_ref, own_ref, other_ref = u_buffers
    if do_v:
        v_ref, product_ref, sum_ref = refs
        v_arrivals = fetch([v_hbm], [v_ref], steps, rows)
        sum_ref[...] = jnp.zeros_like(sum_ref)

    pad = jnp.zeros((16, 256), F32)
    if do_u:
        for q, ref in enumerate(reach_refs):
            for j in range(2):
                x = ref[j].astype(F32)
                re, im = x[:24], x[24:]
                xa_ref[q * 2 + j] = jnp.concatenate([re, im, pad], axis=0).T.astype(BF)
                xb_ref[q * 2 + j] = jnp.concatenate([-im, re, pad], axis=0).T.astype(BF)
        near_terms = []
        for i in range(clusters_dev):
            near_arrivals[i][0].wait()
            total = jnp.zeros((256, 64), F32)
            for k in range(near_ref.shape[1]):
                at = i + offset_ref[i, k] + 2
                total += dot(near_ref[i, k, 0], xa_ref[at]) + dot(near_ref[i, k, 1], xb_ref[at])
            near_terms.append(total.T[:48])
        totals = [jnp.zeros((192, 256), F32) for w in range(2)]
        for step in range(steps):
            for copy in u_arrivals[step]:
                copy.wait()
            at = slice(step * rows, step * rows + rows)
            turned = c_ref[at].astype(F32).T
            for s in range(2):
                base = turned[s * 64 : s * 64 + 48]
                weights = jnp.concatenate(
                    [
                        (base * turned[s * 64 + 48 + o : s * 64 + 49 + o]).astype(BF)
                        for o in range(4)
                    ],
                    axis=0,
                )
                lanes = slice(s * 256, s * 256 + 256)
                totals[0] += dot(weights, own_ref[at, lanes])
                totals[1] += dot(weights, other_ref[at, lanes])
        first_core = core_ref[0] == 0
        clusters = []
        for o in range(4):
            halves = []
            for w in range(2):
                z = totals[w][o * 48 : o * 48 + 48]
                re = z[:24, :128] - z[24:, 128:]
                im = z[24:, :128] + z[:24, 128:]
                halves.append(jnp.concatenate([re, im], axis=0))
            x = jnp.concatenate(
                [
                    jnp.where(first_core, halves[0], halves[1]),
                    jnp.where(first_core, halves[1], halves[0]),
                ],
                axis=1,
            )
            clusters.append(x + near_terms[o])
    else:
        clusters = [field_ref[:, m * 256 : m * 256 + 256] for m in range(4)]

    if not do_v:
        for o in range(4):
            out_ref[:, o * 256 : o * 256 + 256] = clusters[o]
        return

    first, second = [], []
    for m, x in enumerate(clusters):
        rounded = x.astype(BF)
        (low_ref if m < 2 else high_ref)[m % 2] = rounded
        wide = rounded.astype(F32)
        re, im = wide[:24], wide[24:]
        first += [re, im, pad]
        second += [-im, re, pad]
    columns = jnp.concatenate(
        [
            jnp.concatenate(first, axis=0).T.astype(BF),
            jnp.concatenate(second, axis=0).T.astype(BF),
        ],
        axis=0,
    )
    rank_size = sum_ref.shape[1]

    def place(b):
        pair = pl.multiple_of(meta_ref[1, b], 128)
        x = product_ref[b * rank_size : b * rank_size + rank_size, pl.ds(pair, 128)]
        sum_ref[meta_ref[0, b]] = pltpu.roll(x, meta_ref[2, b], 1)

    for copies in v_arrivals:
        for copy in copies:
            copy.wait()
    size = total_rows // PIECES
    for piece in range(PIECES):
        at = slice(piece * size, piece * size + size)
        product_ref[at] = dot(v_ref[at], columns)
        for b in range(piece * size // rank_size, (piece + 1) * size // rank_size):
            place(b)
    half = sum_ref.shape[0] // 2
    lane = lax.broadcasted_iota(jnp.int32, (1, 1, 128), 2)
    both = jnp.where(lane < 64, sum_ref[:half], sum_ref[half:]) + tag_ref[...]
    message_ref[...] = both.reshape(total_rows, 128).astype(BF)


def whole_vmem(count):
    return [pl.BlockSpec(memory_space=pltpu.VMEM)] * count


SCALARS = pl.BlockSpec(memory_space=pltpu.SMEM)


def stage(do_u, do_v, scalars, local, streamed, tags=()):
    steps = STEPS
    in_hbm = pl.BlockSpec(memory_space=pl.ANY)
    scratch = [pltpu.VMEM(x.shape, BF) for x in streamed]
    total_rows = streamed[-1].shape[0]
    copies = 0
    if do_u:
        copies += streamed[0].shape[0] + 3 * steps
        scratch[4:4] = [pltpu.VMEM((8, 256, 64), BF), pltpu.VMEM((8, 256, 64), BF)]
    if do_v:
        rank_size = RANK
        out_shape = [
            jax.ShapeDtypeStruct((total_rows, 128), BF),
            jax.ShapeDtypeStruct((2, 48, 256), BF),
            jax.ShapeDtypeStruct((2, 48, 256), BF),
        ]
        out_specs = whole_vmem(3)
        scratch += [
            pltpu.VMEM((total_rows, 256), F32),
            pltpu.VMEM((2 * (total_rows // rank_size), rank_size, 128), F32),
        ]
        copies += steps
    else:
        out_shape = jax.ShapeDtypeStruct((48, 1024), F32)
        out_specs = whole_vmem(1)[0]
    return pl.pallas_call(
        functools.partial(stage_kernel, do_u, do_v, steps),
        in_specs=[SCALARS] * 3
        + whole_vmem(len(local))
        + [in_hbm] * len(streamed)
        + whole_vmem(len(tags)),
        out_specs=out_specs,
        out_shape=out_shape,
        scratch_shapes=scratch + [pltpu.SemaphoreType.DMA((copies,))],
        compiler_params=pltpu.CompilerParams(vmem_limit_bytes=STAGE_LIMIT),
        cost_estimate=pl.CostEstimate(
            flops=4_000_000_000, bytes_accessed=1_000_000, transcendentals=0
        ),
    )(*scalars, *local, *streamed, *tags)


def place_u(dest, far_u, count):
    return pl.pallas_call(
        place_u_kernel,
        in_specs=[SCALARS, pl.BlockSpec(memory_space=pl.ANY)],
        out_specs=pl.BlockSpec(memory_space=pltpu.VMEM),
        out_shape=jax.ShapeDtypeStruct((count, far_u.shape[2], 4 * far_u.shape[3]), BF),
        scratch_shapes=[
            pltpu.VMEM(far_u.shape, BF),
            pltpu.SMEM((count,), jnp.int32),
            pltpu.SemaphoreType.DMA,
        ],
        compiler_params=pltpu.CompilerParams(vmem_limit_bytes=SETUP_LIMIT),
    )(dest, far_u)


def on_device(
    source_field,
    near_blocks,
    near_offsets,
    far_v,
    far_u,
    far_rank,
    far_col_local,
    far_dest,
    far_row_local,
):
    parts, rhs_dev, panels_dev = source_field.shape
    rank_size = far_v.shape[2]
    count = lax.axis_size("row")
    forward = [(i, i + 1) for i in range(count - 1)]
    backward = [(i + 1, i) for i in range(count - 1)]
    core = lax.axis_index("rhs").astype(jnp.int32).reshape(1)
    dest = far_dest.reshape(-1)

    def exchange(x):
        return lax.all_to_all(x, "row", split_axis=0, concat_axis=0, tiled=True)

    u_own = exchange(place_u(dest, far_u, count))
    order = jnp.arange(dest.shape[0], dtype=jnp.int32)
    earlier = (dest[None, :] == dest[:, None]) & (order[None, :] < order[:, None])
    slot = jnp.sum(earlier.astype(jnp.int32), axis=1)
    meta = jnp.stack(
        [
            slot * count + dest,
            far_col_local // 2 * 128,
            (far_col_local % 2 != slot).astype(jnp.int32) * 64,
        ]
    )
    tag_lane = slot * 64 + 48 + far_row_local
    spread = (
        (jnp.arange(count)[:, None, None] == dest[None, None, :])
        & (jnp.arange(128)[None, :, None] == tag_lane[None, None, :])
    ).astype(F32)
    tags = [jnp.sum(spread, axis=2)[:, None, :]]
    scalars = [core, meta, near_offsets]
    kept = jnp.arange(rank_size, dtype=jnp.int32)[None, :] < far_rank[:, None]
    v_rows = jnp.where(kept[:, :, None, None], far_v.transpose(0, 2, 1, 3), jnp.zeros((), BF))
    v_rows = v_rows.reshape(dest.shape[0] * rank_size, -1)
    field = source_field.reshape(parts * rhs_dev, panels_dev)
    message, low, high = stage(False, True, scalars, [field], [v_rows], tags)
    for application in range(APPS):
        left = lax.ppermute(high, "row", forward)
        right = lax.ppermute(low, "row", backward)
        if application == 0:
            u_own, message = lax.optimization_barrier((u_own, message))
            u_own = u_own.reshape(count * rank_size, -1)
            u_other = lax.ppermute(u_own, "rhs", [(0, 1), (1, 0)])
        arrived = exchange(message.reshape(count, rank_size, 128)).reshape(-1, 128)
        reach = [left, low, high, right]
        streamed = [near_blocks, arrived, u_own, u_other]
        if application < APPS - 1:
            message, low, high = stage(
                True, True, scalars, reach, streamed + [v_rows], tags
            )
    result = stage(True, False, scalars, reach, streamed)
    return result.reshape(parts, rhs_dev, panels_dev)


def solution(mesh):
    return jax.shard_map(
        on_device,
        mesh=mesh,
        in_specs=(
            P(None, "rhs", "row"),
            P("row", None, None, None, None),
            P("row", None),
            P("row", None, None, None),
            P("row", None, None, "rhs"),
            P("row"),
            P("row"),
            P("row", None),
            P("row"),
        ),
        out_specs=P(None, "rhs", "row"),
        check_vma=False,
    )
```

```python
import functools

import jax
import jax.numpy as jnp
from jax import lax
from jax.experimental import pallas as pl
from jax.experimental.pallas import tpu as pltpu
from jax.sharding import PartitionSpec as P

APPS = 4
BF = jnp.bfloat16
F32 = jnp.float32
SETUP_LIMIT = 60 * 1024 * 1024
STAGE_LIMIT = 50 * 1024 * 1024
STEPS = 3
PIECES = 16
RANK = 24
HALO = ((0, -2), (0, -1), (1, -2), (2, 2), (3, 1), (3, 2))


def dot(a, b):
    return jnp.dot(a, b, preferred_element_type=F32)


def next_slot(count_ref, destination):
    slot = count_ref[destination]
    count_ref[destination] = slot + 1
    return slot


def clear_counts(count_ref, count):
    def body(i, carry):
        count_ref[i] = 0
        return carry

    lax.fori_loop(0, count, body, 0)


def place_u_kernel(dest_ref, u_hbm, out_ref, u_ref, count_ref, sem_ref):
    arrival = pltpu.make_async_copy(u_hbm, u_ref, sem_ref)
    arrival.start()
    clear_counts(count_ref, out_ref.shape[0])
    out_ref[...] = jnp.zeros_like(out_ref)
    half = u_ref.shape[3]
    arrival.wait()

    def body(b, carry):
        d = dest_ref[b]
        s = next_slot(count_ref, d)
        for c in range(2):
            lane = pl.multiple_of(s * (2 * half) + c * half, half)
            out_ref[d, :, pl.ds(lane, half)] = u_ref[b, c]
        return carry

    lax.fori_loop(0, u_ref.shape[0], body, 0, unroll=8)


def complex_columns(x):
    x = x.astype(F32)
    re, im = x[:24], x[24:]
    pad = jnp.zeros((16, x.shape[1]), F32)
    first = jnp.concatenate([re, im, pad], axis=0).T.astype(BF)
    second = jnp.concatenate([-im, re, pad], axis=0).T.astype(BF)
    return first, second


def near_own_kernel(
    offset_ref, low_ref, high_ref, near_hbm, out_ref, near_ref, xa_ref, xb_ref, sem_ref
):
    clusters = near_ref.shape[0]
    copies = [
        pltpu.make_async_copy(near_hbm.at[i], near_ref.at[i], sem_ref.at[i])
        for i in range(clusters)
    ]
    for copy in copies:
        copy.start()
    for j in range(clusters):
        xa_ref[j], xb_ref[j] = complex_columns((low_ref if j < 2 else high_ref)[j % 2])
    xa_ref[clusters] = jnp.zeros(xa_ref.shape[1:], BF)
    xb_ref[clusters] = jnp.zeros(xb_ref.shape[1:], BF)
    for i in range(clusters):
        copies[i].wait()
        total = jnp.zeros((256, 64), F32)
        for k in range(near_ref.shape[1]):
            at = i + offset_ref[i, k]
            at = jnp.where((at >= 0) & (at < clusters), at, clusters)
            total += dot(near_ref[i, k, 0], xa_ref[at]) + dot(near_ref[i, k, 1], xb_ref[at])
        out_ref[:, i * 256 : i * 256 + 256] = total.T[:48]


def stage_kernel(do_u, do_v, steps, *refs):
    refs = list(refs)
    sem_ref = refs.pop()
    core_ref, meta_ref, halo_ref = refs[:3]
    refs = refs[3:]
    if do_u:
        left_ref, right_ref, own_near_ref, near_hbm = refs[:4]
        u_hbm, refs = refs[4:7], refs[7:]
        total_rows = u_hbm[0].shape[0]
    else:
        field_ref = refs.pop(0)
    if do_v:
        v_hbm, tag_ref = refs[:2]
        refs = refs[2:]
        total_rows = v_hbm.shape[0]
        message_ref, low_ref, high_ref = refs[:3]
        refs = refs[3:]
    else:
        out_ref = refs.pop(0)
    rows = total_rows // steps
    started = []

    def fetch(sources, targets, pieces, size):
        arrivals = []
        for piece in range(pieces):
            at = pl.ds(piece * size, size)
            copies = []
            for source, target in zip(sources, targets):
                copy = pltpu.make_async_copy(
                    source.at[at], target.at[at], sem_ref.at[len(started)]
                )
                copy.start()
                started.append(copy)
                copies.append(copy)
            arrivals.append(copies)
        return arrivals

    if do_u:
        near_ref, u_buffers, xa_ref, xb_ref = refs[0], refs[1:4], refs[4], refs[5]
        refs = refs[6:]
        near_arrivals = []
        for j, (i, offset) in enumerate(HALO):
            copy = pltpu.make_async_copy(
                near_hbm.at[i, halo_ref[0, j]], near_ref.at[j], sem_ref.at[len(started)]
            )
            copy.start()
            started.append(copy)
            near_arrivals.append(copy)
        u_arrivals = fetch(u_hbm, u_buffers, steps, rows)
        c_ref, own_ref, other_ref = u_buffers
    if do_v:
        v_ref, product_ref, sum_ref = refs
        v_arrivals = fetch([v_hbm], [v_ref], steps, rows)
        sum_ref[...] = jnp.zeros_like(sum_ref)

    pad = jnp.zeros((16, 256), F32)
    if do_u:
        for q in range(4):
            xa_ref[q], xb_ref[q] = complex_columns((left_ref if q < 2 else right_ref)[q % 2])
        xa_ref[4] = jnp.zeros(xa_ref.shape[1:], BF)
        xb_ref[4] = jnp.zeros(xb_ref.shape[1:], BF)
        sums = [jnp.zeros((256, 64), F32) for o in range(4)]
        for j, (i, offset) in enumerate(HALO):
            near_arrivals[j].wait()
            at = i + offset + 2 if offset < 0 else i + offset - 2
            at = jnp.where(halo_ref[1, j] == 1, at, 4)
            sums[i] += dot(near_ref[j, 0], xa_ref[at]) + dot(near_ref[j, 1], xb_ref[at])
        near_terms = [
            own_near_ref[:, i * 256 : i * 256 + 256] + sums[i].T[:48] for i in range(4)
        ]
        totals = [jnp.zeros((192, 256), F32) for w in range(2)]
        for step in range(steps):
            for copy in u_arrivals[step]:
                copy.wait()
            at = slice(step * rows, step * rows + rows)
            turned = c_ref[at].astype(F32).T
            for s in range(2):
                base = turned[s * 64 : s * 64 + 48]
                weights = jnp.concatenate(
                    [
                        (base * turned[s * 64 + 48 + o : s * 64 + 49 + o]).astype(BF)
                        for o in range(4)
                    ],
                    axis=0,
                )
                lanes = slice(s * 256, s * 256 + 256)
                totals[0] += dot(weights, own_ref[at, lanes])
                totals[1] += dot(weights, other_ref[at, lanes])
        first_core = core_ref[0] == 0
        clusters = []
        for o in range(4):
            halves = []
            for w in range(2):
                z = totals[w][o * 48 : o * 48 + 48]
                re = z[:24, :128] - z[24:, 128:]
                im = z[24:, :128] + z[:24, 128:]
                halves.append(jnp.concatenate([re, im], axis=0))
            x = jnp.concatenate(
                [
                    jnp.where(first_core, halves[0], halves[1]),
                    jnp.where(first_core, halves[1], halves[0]),
                ],
                axis=1,
            )
            clusters.append(x + near_terms[o])
    else:
        clusters = [field_ref[:, m * 256 : m * 256 + 256] for m in range(4)]

    if not do_v:
        for o in range(4):
            out_ref[:, o * 256 : o * 256 + 256] = clusters[o]
        return

    first, second = [], []
    for m, x in enumerate(clusters):
        rounded = x.astype(BF)
        (low_ref if m < 2 else high_ref)[m % 2] = rounded
        wide = rounded.astype(F32)
        re, im = wide[:24], wide[24:]
        first += [re, im, pad]
        second += [-im, re, pad]
    columns = jnp.concatenate(
        [
            jnp.concatenate(first, axis=0).T.astype(BF),
            jnp.concatenate(second, axis=0).T.astype(BF),
        ],
        axis=0,
    )
    rank_size = sum_ref.shape[1]

    def place(b):
        pair = pl.multiple_of(meta_ref[1, b], 128)
        x = product_ref[b * rank_size : b * rank_size + rank_size, pl.ds(pair, 128)]
        sum_ref[meta_ref[0, b]] = pltpu.roll(x, meta_ref[2, b], 1)

    for copies in v_arrivals:
        for copy in copies:
            copy.wait()
    size = total_rows // PIECES
    for piece in range(PIECES):
        at = slice(piece * size, piece * size + size)
        product_ref[at] = dot(v_ref[at], columns)
        for b in range(piece * size // rank_size, (piece + 1) * size // rank_size):
            place(b)
    half = sum_ref.shape[0] // 2
    lane = lax.broadcasted_iota(jnp.int32, (1, 1, 128), 2)
    both = jnp.where(lane < 64, sum_ref[:half], sum_ref[half:]) + tag_ref[...]
    message_ref[...] = both.reshape(total_rows, 128).astype(BF)


def whole_vmem(count):
    return [pl.BlockSpec(memory_space=pltpu.VMEM)] * count


SCALARS = pl.BlockSpec(memory_space=pltpu.SMEM)


def stage(do_u, do_v, scalars, local, streamed, tags=()):
    steps = STEPS
    in_hbm = pl.BlockSpec(memory_space=pl.ANY)
    scratch = [pltpu.VMEM(x.shape, BF) for x in streamed]
    total_rows = streamed[-1].shape[0]
    copies = 0
    if do_u:
        copies += len(HALO) + 3 * steps
        scratch[0] = pltpu.VMEM((len(HALO),) + streamed[0].shape[2:], BF)
        scratch[4:4] = [pltpu.VMEM((5, 256, 64), BF), pltpu.VMEM((5, 256, 64), BF)]
    if do_v:
        rank_size = RANK
        out_shape = [
            jax.ShapeDtypeStruct((total_rows, 128), BF),
            jax.ShapeDtypeStruct((2, 48, 256), BF),
            jax.ShapeDtypeStruct((2, 48, 256), BF),
        ]
        out_specs = whole_vmem(3)
        scratch += [
            pltpu.VMEM((total_rows, 256), F32),
            pltpu.VMEM((2 * (total_rows // rank_size), rank_size, 128), F32),
        ]
        copies += steps
    else:
        out_shape = jax.ShapeDtypeStruct((48, 1024), F32)
        out_specs = whole_vmem(1)[0]
    return pl.pallas_call(
        functools.partial(stage_kernel, do_u, do_v, steps),
        in_specs=[SCALARS] * 3
        + whole_vmem(len(local))
        + [in_hbm] * len(streamed)
        + whole_vmem(len(tags)),
        out_specs=out_specs,
        out_shape=out_shape,
        scratch_shapes=scratch + [pltpu.SemaphoreType.DMA((copies,))],
        compiler_params=pltpu.CompilerParams(vmem_limit_bytes=STAGE_LIMIT),
        cost_estimate=pl.CostEstimate(
            flops=4_000_000_000, bytes_accessed=1_000_000, transcendentals=0
        ),
    )(*scalars, *local, *streamed, *tags)


def near_own(offsets, low, high, blocks):
    clusters = blocks.shape[0]
    return pl.pallas_call(
        near_own_kernel,
        in_specs=[SCALARS] + whole_vmem(2) + [pl.BlockSpec(memory_space=pl.ANY)],
        out_specs=whole_vmem(1)[0],
        out_shape=jax.ShapeDtypeStruct((48, clusters * 256), F32),
        scratch_shapes=[
            pltpu.VMEM(blocks.shape, BF),
            pltpu.VMEM((clusters + 1, 256, 64), BF),
            pltpu.VMEM((clusters + 1, 256, 64), BF),
            pltpu.SemaphoreType.DMA((clusters,)),
        ],
        compiler_params=pltpu.CompilerParams(vmem_limit_bytes=STAGE_LIMIT),
        cost_estimate=pl.CostEstimate(
            flops=3_000_000_000, bytes_accessed=4_500_000, transcendentals=0
        ),
    )(offsets, low, high, blocks)


def place_u(dest, far_u, count):
    return pl.pallas_call(
        place_u_kernel,
        in_specs=[SCALARS, pl.BlockSpec(memory_space=pl.ANY)],
        out_specs=pl.BlockSpec(memory_space=pltpu.VMEM),
        out_shape=jax.ShapeDtypeStruct((count, far_u.shape[2], 4 * far_u.shape[3]), BF),
        scratch_shapes=[
            pltpu.VMEM(far_u.shape, BF),
            pltpu.SMEM((count,), jnp.int32),
            pltpu.SemaphoreType.DMA,
        ],
        compiler_params=pltpu.CompilerParams(vmem_limit_bytes=SETUP_LIMIT),
    )(dest, far_u)


def on_device(
    source_field,
    near_blocks,
    near_offsets,
    far_v,
    far_u,
    far_rank,
    far_col_local,
    far_dest,
    far_row_local,
):
    parts, rhs_dev, panels_dev = source_field.shape
    rank_size = far_v.shape[2]
    count = lax.axis_size("row")
    forward = [(i, i + 1) for i in range(count - 1)]
    backward = [(i + 1, i) for i in range(count - 1)]
    core = lax.axis_index("rhs").astype(jnp.int32).reshape(1)
    dest = far_dest.reshape(-1)

    def exchange(x):
        return lax.all_to_all(x, "row", split_axis=0, concat_axis=0, tiled=True)

    u_own = exchange(place_u(dest, far_u, count))
    order = jnp.arange(dest.shape[0], dtype=jnp.int32)
    earlier = (dest[None, :] == dest[:, None]) & (order[None, :] < order[:, None])
    slot = jnp.sum(earlier.astype(jnp.int32), axis=1)
    meta = jnp.stack(
        [
            slot * count + dest,
            far_col_local // 2 * 128,
            (far_col_local % 2 != slot).astype(jnp.int32) * 64,
        ]
    )
    tag_lane = slot * 64 + 48 + far_row_local
    spread = (
        (jnp.arange(count)[:, None, None] == dest[None, None, :])
        & (jnp.arange(128)[None, :, None] == tag_lane[None, None, :])
    ).astype(F32)
    tags = [jnp.sum(spread, axis=2)[:, None, :]]
    matches = jnp.stack([near_offsets[i] == offset for i, offset in HALO])
    positions = jnp.arange(matches.shape[1], dtype=jnp.int32)
    halo = jnp.stack(
        [
            jnp.sum(jnp.where(matches, positions[None, :], 0), axis=1),
            jnp.sum(matches.astype(jnp.int32), axis=1),
        ]
    )
    scalars = [core, meta, halo]
    kept = jnp.arange(rank_size, dtype=jnp.int32)[None, :] < far_rank[:, None]
    v_rows = jnp.where(kept[:, :, None, None], far_v.transpose(0, 2, 1, 3), jnp.zeros((), BF))
    v_rows = v_rows.reshape(dest.shape[0] * rank_size, -1)
    field = source_field.reshape(parts * rhs_dev, panels_dev)
    message, low, high = stage(False, True, scalars, [field], [v_rows], tags)
    for application in range(APPS):
        left = lax.ppermute(high, "row", forward)
        right = lax.ppermute(low, "row", backward)
        if application == 0:
            u_own, message = lax.optimization_barrier((u_own, message))
            u_own = u_own.reshape(count * rank_size, -1)
            u_other = lax.ppermute(u_own, "rhs", [(0, 1), (1, 0)])
        arrived = exchange(message.reshape(count, rank_size, 128)).reshape(-1, 128)
        reach = [left, right, near_own(near_offsets, low, high, near_blocks)]
        streamed = [near_blocks, arrived, u_own, u_other]
        if application < APPS - 1:
            message, low, high = stage(
                True, True, scalars, reach, streamed + [v_rows], tags
            )
    result = stage(True, False, scalars, reach, streamed)
    return result.reshape(parts, rhs_dev, panels_dev)


def solution(mesh):
    return jax.shard_map(
        on_device,
        mesh=mesh,
        in_specs=(
            P(None, "rhs", "row"),
            P("row", None, None, None, None),
            P("row", None),
            P("row", None, None, None),
            P("row", None, None, "rhs"),
            P("row"),
            P("row"),
            P("row", None),
            P("row"),
        ),
        out_specs=P(None, "rhs", "row"),
        check_vma=False,
    )
```

```python
import functools

import jax
import jax.numpy as jnp
from jax import lax
from jax.experimental import pallas as pl
from jax.experimental.pallas import tpu as pltpu
from jax.sharding import PartitionSpec as P

APPS = 4
BF = jnp.bfloat16
F32 = jnp.float32
SETUP_LIMIT = 60 * 1024 * 1024
STAGE_LIMIT = 50 * 1024 * 1024
STEPS = 3
PIECES = 16
RANK = 24
HALO = ((0, -2), (0, -1), (1, -2), (2, 2), (3, 1), (3, 2))


def dot(a, b):
    return jnp.dot(a, b, preferred_element_type=F32)


def next_slot(count_ref, destination):
    slot = count_ref[destination]
    count_ref[destination] = slot + 1
    return slot


def clear_counts(count_ref, count):
    def body(i, carry):
        count_ref[i] = 0
        return carry

    lax.fori_loop(0, count, body, 0)


def place_u_kernel(dest_ref, u_hbm, out_ref, u_ref, count_ref, sem_ref):
    arrival = pltpu.make_async_copy(u_hbm, u_ref, sem_ref)
    arrival.start()
    clear_counts(count_ref, out_ref.shape[0])
    out_ref[...] = jnp.zeros_like(out_ref)
    half = u_ref.shape[3]
    arrival.wait()

    def body(b, carry):
        d = dest_ref[b]
        s = next_slot(count_ref, d)
        for c in range(2):
            lane = pl.multiple_of(s * (2 * half) + c * half, half)
            out_ref[d, :, pl.ds(lane, half)] = u_ref[b, c]
        return carry

    lax.fori_loop(0, u_ref.shape[0], body, 0, unroll=8)


def complex_columns(x):
    x = x.astype(F32)
    re, im = x[:24], x[24:]
    pad = jnp.zeros((16, x.shape[1]), F32)
    first = jnp.concatenate([re, im, pad], axis=0).T.astype(BF)
    second = jnp.concatenate([-im, re, pad], axis=0).T.astype(BF)
    return first, second


def near_own_kernel(
    offset_ref, low_ref, high_ref, near_hbm, out_ref, near_ref, xa_ref, xb_ref, sem_ref
):
    clusters = near_ref.shape[0]
    copies = [
        pltpu.make_async_copy(near_hbm.at[i], near_ref.at[i], sem_ref.at[i])
        for i in range(clusters)
    ]
    for copy in copies:
        copy.start()
    for j in range(clusters):
        xa_ref[j], xb_ref[j] = complex_columns((low_ref if j < 2 else high_ref)[j % 2])
    xa_ref[clusters] = jnp.zeros(xa_ref.shape[1:], BF)
    xb_ref[clusters] = jnp.zeros(xb_ref.shape[1:], BF)
    for i in range(clusters):
        copies[i].wait()
        total = jnp.zeros((256, 64), F32)
        for k in range(near_ref.shape[1]):
            at = i + offset_ref[i, k]
            at = jnp.where((at >= 0) & (at < clusters), at, clusters)
            total += dot(near_ref[i, k, 0], xa_ref[at]) + dot(near_ref[i, k, 1], xb_ref[at])
        out_ref[:, i * 256 : i * 256 + 256] = total.T[:48]


def stage_kernel(do_u, do_v, steps, *refs):
    refs = list(refs)
    sem_ref = refs.pop()
    core_ref, meta_ref, halo_ref = refs[:3]
    refs = refs[3:]
    if do_u:
        left_ref, right_ref, own_near_ref, near_hbm = refs[:4]
        u_hbm, refs = refs[4:7], refs[7:]
        total_rows = u_hbm[0].shape[0]
    else:
        field_ref = refs.pop(0)
    if do_v:
        v_hbm, tag_ref = refs[:2]
        refs = refs[2:]
        total_rows = v_hbm.shape[0]
        message_ref, low_ref, high_ref = refs[:3]
        refs = refs[3:]
    else:
        out_ref = refs.pop(0)
    rows = total_rows // steps
    started = []

    def fetch(sources, targets, pieces, size):
        arrivals = []
        for piece in range(pieces):
            at = pl.ds(piece * size, size)
            copies = []
            for source, target in zip(sources, targets):
                copy = pltpu.make_async_copy(
                    source.at[at], target.at[at], sem_ref.at[len(started)]
                )
                copy.start()
                started.append(copy)
                copies.append(copy)
            arrivals.append(copies)
        return arrivals

    if do_u:
        near_ref, u_buffers, xa_ref, xb_ref = refs[0], refs[1:4], refs[4], refs[5]
        refs = refs[6:]
        near_arrivals = []
        for j, (i, offset) in enumerate(HALO):
            copy = pltpu.make_async_copy(
                near_hbm.at[i, halo_ref[0, j]], near_ref.at[j], sem_ref.at[len(started)]
            )
            copy.start()
            started.append(copy)
            near_arrivals.append(copy)
        u_arrivals = fetch(u_hbm, u_buffers, steps, rows)
        c_ref, own_ref, other_ref = u_buffers
    if do_v:
        v_ref, product_ref, sum_ref = refs
        v_arrivals = fetch([v_hbm], [v_ref], steps, rows)
        sum_ref[...] = jnp.zeros_like(sum_ref)

    pad = jnp.zeros((16, 256), F32)
    if do_u:
        for q in range(4):
            xa_ref[q], xb_ref[q] = complex_columns((left_ref if q < 2 else right_ref)[q % 2])
        xa_ref[4] = jnp.zeros(xa_ref.shape[1:], BF)
        xb_ref[4] = jnp.zeros(xb_ref.shape[1:], BF)
        sums = [jnp.zeros((256, 64), F32) for o in range(4)]
        for j, (i, offset) in enumerate(HALO):
            near_arrivals[j].wait()
            at = i + offset + 2 if offset < 0 else i + offset - 2
            at = jnp.where(halo_ref[1, j] == 1, at, 4)
            sums[i] += dot(near_ref[j, 0], xa_ref[at]) + dot(near_ref[j, 1], xb_ref[at])
        near_terms = [
            own_near_ref[:, i * 256 : i * 256 + 256] + sums[i].T[:48] for i in range(4)
        ]
        totals = [jnp.zeros((192, 256), F32) for w in range(2)]
        for step in range(steps):
            for copy in u_arrivals[step]:
                copy.wait()
            at = slice(step * rows, step * rows + rows)
            turned = c_ref[at].astype(F32).T
            for s in range(2):
                base = turned[s * 64 : s * 64 + 48]
                weights = jnp.concatenate(
                    [
                        (base * turned[s * 64 + 48 + o : s * 64 + 49 + o]).astype(BF)
                        for o in range(4)
                    ],
                    axis=0,
                )
                lanes = slice(s * 256, s * 256 + 256)
                totals[0] += dot(weights, own_ref[at, lanes])
                totals[1] += dot(weights, other_ref[at, lanes])
        first_core = core_ref[0] == 0
        clusters = []
        for o in range(4):
            halves = []
            for w in range(2):
                z = totals[w][o * 48 : o * 48 + 48]
                re = z[:24, :128] - z[24:, 128:]
                im = z[24:, :128] + z[:24, 128:]
                halves.append(jnp.concatenate([re, im], axis=0))
            x = jnp.concatenate(
                [
                    jnp.where(first_core, halves[0], halves[1]),
                    jnp.where(first_core, halves[1], halves[0]),
                ],
                axis=1,
            )
            clusters.append(x + near_terms[o])
    else:
        clusters = [field_ref[:, m * 256 : m * 256 + 256] for m in range(4)]

    if not do_v:
        for o in range(4):
            out_ref[:, o * 256 : o * 256 + 256] = clusters[o]
        return

    first, second = [], []
    for m, x in enumerate(clusters):
        rounded = x.astype(BF)
        (low_ref if m < 2 else high_ref)[m % 2] = rounded
        wide = rounded.astype(F32)
        re, im = wide[:24], wide[24:]
        first += [re, im, pad]
        second += [-im, re, pad]
    columns = jnp.concatenate(
        [
            jnp.concatenate(first, axis=0).T.astype(BF),
            jnp.concatenate(second, axis=0).T.astype(BF),
        ],
        axis=0,
    )
    rank_size = sum_ref.shape[1]

    def place(b):
        pair = pl.multiple_of(meta_ref[1, b], 128)
        x = product_ref[b * rank_size : b * rank_size + rank_size, pl.ds(pair, 128)]
        sum_ref[meta_ref[0, b]] = pltpu.roll(x, meta_ref[2, b], 1)

    for copies in v_arrivals:
        for copy in copies:
            copy.wait()
    size = total_rows // PIECES
    for piece in range(PIECES):
        at = slice(piece * size, piece * size + size)
        product_ref[at] = dot(v_ref[at], columns)
        for b in range(piece * size // rank_size, (piece + 1) * size // rank_size):
            place(b)
    half = sum_ref.shape[0] // 2
    lane = lax.broadcasted_iota(jnp.int32, (1, 1, 128), 2)
    both = jnp.where(lane < 64, sum_ref[:half], sum_ref[half:]) + tag_ref[...]
    message_ref[...] = both.reshape(total_rows, 128).astype(BF)


def whole_vmem(count):
    return [pl.BlockSpec(memory_space=pltpu.VMEM)] * count


SCALARS = pl.BlockSpec(memory_space=pltpu.SMEM)


def stage(do_u, do_v, scalars, local, streamed, tags=()):
    steps = STEPS
    in_hbm = pl.BlockSpec(memory_space=pl.ANY)
    scratch = [pltpu.VMEM(x.shape, BF) for x in streamed]
    total_rows = streamed[-1].shape[0]
    copies = 0
    if do_u:
        copies += len(HALO) + 3 * steps
        scratch[0] = pltpu.VMEM((len(HALO),) + streamed[0].shape[2:], BF)
        scratch[4:4] = [pltpu.VMEM((5, 256, 64), BF), pltpu.VMEM((5, 256, 64), BF)]
    if do_v:
        rank_size = RANK
        out_shape = [
            jax.ShapeDtypeStruct((total_rows, 128), BF),
            jax.ShapeDtypeStruct((2, 48, 256), BF),
            jax.ShapeDtypeStruct((2, 48, 256), BF),
        ]
        out_specs = whole_vmem(3)
        scratch += [
            pltpu.VMEM((total_rows, 256), F32),
            pltpu.VMEM((2 * (total_rows // rank_size), rank_size, 128), F32),
        ]
        copies += steps
    else:
        out_shape = jax.ShapeDtypeStruct((48, 1024), F32)
        out_specs = whole_vmem(1)[0]
    return pl.pallas_call(
        functools.partial(stage_kernel, do_u, do_v, steps),
        in_specs=[SCALARS] * 3
        + whole_vmem(len(local))
        + [in_hbm] * len(streamed)
        + whole_vmem(len(tags)),
        out_specs=out_specs,
        out_shape=out_shape,
        scratch_shapes=scratch + [pltpu.SemaphoreType.DMA((copies,))],
        compiler_params=pltpu.CompilerParams(vmem_limit_bytes=STAGE_LIMIT),
        cost_estimate=pl.CostEstimate(
            flops=4_000_000_000, bytes_accessed=1_000_000, transcendentals=0
        ),
    )(*scalars, *local, *streamed, *tags)


def near_own(offsets, low, high, blocks):
    clusters = blocks.shape[0]
    return pl.pallas_call(
        near_own_kernel,
        in_specs=[SCALARS] + whole_vmem(2) + [pl.BlockSpec(memory_space=pl.ANY)],
        out_specs=whole_vmem(1)[0],
        out_shape=jax.ShapeDtypeStruct((48, clusters * 256), F32),
        scratch_shapes=[
            pltpu.VMEM(blocks.shape, BF),
            pltpu.VMEM((clusters + 1, 256, 64), BF),
            pltpu.VMEM((clusters + 1, 256, 64), BF),
            pltpu.SemaphoreType.DMA((clusters,)),
        ],
        compiler_params=pltpu.CompilerParams(vmem_limit_bytes=STAGE_LIMIT),
        cost_estimate=pl.CostEstimate(
            flops=3_000_000_000, bytes_accessed=4_500_000, transcendentals=0
        ),
    )(offsets, low, high, blocks)


def place_u(dest, far_u, count):
    return pl.pallas_call(
        place_u_kernel,
        in_specs=[SCALARS, pl.BlockSpec(memory_space=pl.ANY)],
        out_specs=pl.BlockSpec(memory_space=pltpu.VMEM),
        out_shape=jax.ShapeDtypeStruct((count, far_u.shape[2], 4 * far_u.shape[3]), BF),
        scratch_shapes=[
            pltpu.VMEM(far_u.shape, BF),
            pltpu.SMEM((count,), jnp.int32),
            pltpu.SemaphoreType.DMA,
        ],
        compiler_params=pltpu.CompilerParams(vmem_limit_bytes=SETUP_LIMIT),
    )(dest, far_u)


def on_device(
    source_field,
    near_blocks,
    near_offsets,
    far_v,
    far_u,
    far_rank,
    far_col_local,
    far_dest,
    far_row_local,
):
    parts, rhs_dev, panels_dev = source_field.shape
    rank_size = far_v.shape[2]
    count = lax.axis_size("row")
    forward = [(i, i + 1) for i in range(count - 1)]
    backward = [(i + 1, i) for i in range(count - 1)]
    core = lax.axis_index("rhs").astype(jnp.int32).reshape(1)
    dest = far_dest.reshape(-1)

    def exchange(x):
        return lax.all_to_all(x, "row", split_axis=0, concat_axis=0, tiled=True)

    u_own = exchange(place_u(dest, far_u, count))
    order = jnp.arange(dest.shape[0], dtype=jnp.int32)
    earlier = (dest[None, :] == dest[:, None]) & (order[None, :] < order[:, None])
    slot = jnp.sum(earlier.astype(jnp.int32), axis=1)
    meta = jnp.stack(
        [
            slot * count + dest,
            far_col_local // 2 * 128,
            (far_col_local % 2 != slot).astype(jnp.int32) * 64,
        ]
    )
    tag_lane = slot * 64 + 48 + far_row_local
    spread = (
        (jnp.arange(count)[:, None, None] == dest[None, None, :])
        & (jnp.arange(128)[None, :, None] == tag_lane[None, None, :])
    ).astype(F32)
    tags = [jnp.sum(spread, axis=2)[:, None, :]]
    matches = jnp.stack([near_offsets[i] == offset for i, offset in HALO])
    positions = jnp.arange(matches.shape[1], dtype=jnp.int32)
    halo = jnp.stack(
        [
            jnp.sum(jnp.where(matches, positions[None, :], 0), axis=1),
            jnp.sum(matches.astype(jnp.int32), axis=1),
        ]
    )
    scalars = [core, meta, halo]
    kept = jnp.arange(rank_size, dtype=jnp.int32)[None, :] < far_rank[:, None]
    v_rows = jnp.where(kept[:, :, None, None], far_v.transpose(0, 2, 1, 3), jnp.zeros((), BF))
    v_rows = v_rows.reshape(dest.shape[0] * rank_size, -1)
    field = source_field.reshape(parts * rhs_dev, panels_dev)
    message, low, high = stage(False, True, scalars, [field], [v_rows], tags)
    for application in range(APPS):
        left = lax.ppermute(high, "row", forward)
        right = lax.ppermute(low, "row", backward)
        if application == 0:
            u_own, message = lax.optimization_barrier((u_own, message))
            u_own = u_own.reshape(count * rank_size, -1)
        arrived = exchange(message.reshape(count, rank_size, 128)).reshape(-1, 128)
        near_term = near_own(near_offsets, low, high, near_blocks)
        if application == 0:
            u_own, near_term = lax.optimization_barrier((u_own, near_term))
            u_other = lax.ppermute(u_own, "rhs", [(0, 1), (1, 0)])
        reach = [left, right, near_term]
        streamed = [near_blocks, arrived, u_own, u_other]
        if application < APPS - 1:
            message, low, high = stage(
                True, True, scalars, reach, streamed + [v_rows], tags
            )
    result = stage(True, False, scalars, reach, streamed)
    return result.reshape(parts, rhs_dev, panels_dev)


def solution(mesh):
    return jax.shard_map(
        on_device,
        mesh=mesh,
        in_specs=(
            P(None, "rhs", "row"),
            P("row", None, None, None, None),
            P("row", None),
            P("row", None, None, None),
            P("row", None, None, "rhs"),
            P("row"),
            P("row"),
            P("row", None),
            P("row"),
        ),
        out_specs=P(None, "rhs", "row"),
        check_vma=False,
    )
```

```python
import functools

import jax
import jax.numpy as jnp
from jax import lax
from jax.experimental import pallas as pl
from jax.experimental.pallas import tpu as pltpu
from jax.sharding import PartitionSpec as P

APPS = 4
BF = jnp.bfloat16
F32 = jnp.float32
SETUP_LIMIT = 60 * 1024 * 1024
STAGE_LIMIT = 50 * 1024 * 1024
STEPS = 3
PIECES = 16
RANK = 24
HALO = ((0, -2), (0, -1), (1, -2), (2, 2), (3, 1), (3, 2))


def dot(a, b):
    return jnp.dot(a, b, preferred_element_type=F32)


def next_slot(count_ref, destination):
    slot = count_ref[destination]
    count_ref[destination] = slot + 1
    return slot


def clear_counts(count_ref, count):
    def body(i, carry):
        count_ref[i] = 0
        return carry

    lax.fori_loop(0, count, body, 0)


def place_u_kernel(dest_ref, u_hbm, out_ref, u_ref, count_ref, sem_ref):
    arrival = pltpu.make_async_copy(u_hbm, u_ref, sem_ref)
    arrival.start()
    clear_counts(count_ref, out_ref.shape[0])
    out_ref[...] = jnp.zeros_like(out_ref)
    half = u_ref.shape[3]
    arrival.wait()

    def body(b, carry):
        d = dest_ref[b]
        s = next_slot(count_ref, d)
        for c in range(2):
            lane = pl.multiple_of(s * (2 * half) + c * half, half)
            out_ref[d, :, pl.ds(lane, half)] = u_ref[b, c]
        return carry

    lax.fori_loop(0, u_ref.shape[0], body, 0, unroll=8)


def complex_columns(x):
    x = x.astype(F32)
    re, im = x[:24], x[24:]
    pad = jnp.zeros((16, x.shape[1]), F32)
    first = jnp.concatenate([re, im, pad], axis=0).T.astype(BF)
    second = jnp.concatenate([-im, re, pad], axis=0).T.astype(BF)
    return first, second


def near_own_kernel(
    offset_ref, low_ref, high_ref, near_hbm, out_ref, near_ref, xa_ref, xb_ref, sem_ref
):
    clusters = near_ref.shape[0]
    copies = [
        pltpu.make_async_copy(near_hbm.at[i], near_ref.at[i], sem_ref.at[i])
        for i in range(clusters)
    ]
    for copy in copies:
        copy.start()
    for j in range(clusters):
        xa_ref[j], xb_ref[j] = complex_columns((low_ref if j < 2 else high_ref)[j % 2])
    xa_ref[clusters] = jnp.zeros(xa_ref.shape[1:], BF)
    xb_ref[clusters] = jnp.zeros(xb_ref.shape[1:], BF)
    for i in range(clusters):
        copies[i].wait()
        total = jnp.zeros((256, 64), F32)
        for k in range(near_ref.shape[1]):
            at = i + offset_ref[i, k]
            at = jnp.where((at >= 0) & (at < clusters), at, clusters)
            total += dot(near_ref[i, k, 0], xa_ref[at]) + dot(near_ref[i, k, 1], xb_ref[at])
        out_ref[:, i * 256 : i * 256 + 256] = total.T[:48]


def stage_kernel(do_u, do_v, steps, *refs):
    refs = list(refs)
    sem_ref = refs.pop()
    core_ref, meta_ref, halo_ref = refs[:3]
    refs = refs[3:]
    if do_u:
        left_ref, right_ref, own_near_ref, near_hbm = refs[:4]
        u_hbm, refs = refs[4:7], refs[7:]
        total_rows = u_hbm[0].shape[0]
    else:
        field_ref = refs.pop(0)
    if do_v:
        v_hbm, tag_ref = refs[:2]
        refs = refs[2:]
        total_rows = v_hbm.shape[0]
        message_ref, low_ref, high_ref = refs[:3]
        refs = refs[3:]
    else:
        out_ref = refs.pop(0)
    rows = total_rows // steps
    started = []

    def fetch(sources, targets, pieces, size):
        arrivals = []
        for piece in range(pieces):
            at = pl.ds(piece * size, size)
            copies = []
            for source, target in zip(sources, targets):
                copy = pltpu.make_async_copy(
                    source.at[at], target.at[at], sem_ref.at[len(started)]
                )
                copy.start()
                started.append(copy)
                copies.append(copy)
            arrivals.append(copies)
        return arrivals

    if do_u:
        near_ref, u_buffers, xa_ref, xb_ref = refs[0], refs[1:4], refs[4], refs[5]
        refs = refs[6:]
        near_arrivals = []
        for j, (i, offset) in enumerate(HALO):
            copy = pltpu.make_async_copy(
                near_hbm.at[i, halo_ref[0, j]], near_ref.at[j], sem_ref.at[len(started)]
            )
            copy.start()
            started.append(copy)
            near_arrivals.append(copy)
        u_arrivals = fetch(u_hbm, u_buffers, steps, rows)
        c_ref, own_ref, other_ref = u_buffers
    if do_v:
        v_ref, product_ref, sum_ref = refs
        v_arrivals = fetch([v_hbm], [v_ref], steps, rows)
        sum_ref[...] = jnp.zeros_like(sum_ref)

    pad = jnp.zeros((16, 256), F32)
    if do_u:
        for q in range(4):
            xa_ref[q], xb_ref[q] = complex_columns((left_ref if q < 2 else right_ref)[q % 2])
        xa_ref[4] = jnp.zeros(xa_ref.shape[1:], BF)
        xb_ref[4] = jnp.zeros(xb_ref.shape[1:], BF)
        sums = [jnp.zeros((256, 64), F32) for o in range(4)]
        for j, (i, offset) in enumerate(HALO):
            near_arrivals[j].wait()
            at = i + offset + 2 if offset < 0 else i + offset - 2
            at = jnp.where(halo_ref[1, j] == 1, at, 4)
            sums[i] += dot(near_ref[j, 0], xa_ref[at]) + dot(near_ref[j, 1], xb_ref[at])
        near_terms = [
            own_near_ref[:, i * 256 : i * 256 + 256] + sums[i].T[:48] for i in range(4)
        ]
        totals = [jnp.zeros((192, 256), F32) for w in range(2)]
        for step in range(steps):
            for copy in u_arrivals[step]:
                copy.wait()
            at = slice(step * rows, step * rows + rows)
            turned = c_ref[at].astype(F32).T
            for s in range(2):
                base = turned[s * 64 : s * 64 + 48]
                weights = jnp.concatenate(
                    [
                        (base * turned[s * 64 + 48 + o : s * 64 + 49 + o]).astype(BF)
                        for o in range(4)
                    ],
                    axis=0,
                )
                lanes = slice(s * 256, s * 256 + 256)
                totals[0] += dot(weights, own_ref[at, lanes])
                totals[1] += dot(weights, other_ref[at, lanes])
        first_core = core_ref[0] == 0
        clusters = []
        for o in range(4):
            halves = []
            for w in range(2):
                z = totals[w][o * 48 : o * 48 + 48]
                re = z[:24, :128] - z[24:, 128:]
                im = z[24:, :128] + z[:24, 128:]
                halves.append(jnp.concatenate([re, im], axis=0))
            x = jnp.concatenate(
                [
                    jnp.where(first_core, halves[0], halves[1]),
                    jnp.where(first_core, halves[1], halves[0]),
                ],
                axis=1,
            )
            clusters.append(x + near_terms[o])
    else:
        clusters = [field_ref[:, m * 256 : m * 256 + 256] for m in range(4)]

    if not do_v:
        for o in range(4):
            out_ref[:, o * 256 : o * 256 + 256] = clusters[o]
        return

    first, second = [], []
    for m, x in enumerate(clusters):
        rounded = x.astype(BF)
        (low_ref if m < 2 else high_ref)[m % 2] = rounded
        wide = rounded.astype(F32)
        re, im = wide[:24], wide[24:]
        first += [re, im, pad]
        second += [-im, re, pad]
    columns = jnp.concatenate(
        [
            jnp.concatenate(first, axis=0).T.astype(BF),
            jnp.concatenate(second, axis=0).T.astype(BF),
        ],
        axis=0,
    )
    rank_size = sum_ref.shape[1]

    def place(b):
        pair = pl.multiple_of(meta_ref[1, b], 128)
        x = product_ref[b * rank_size : b * rank_size + rank_size, pl.ds(pair, 128)]
        sum_ref[meta_ref[0, b]] = pltpu.roll(x, meta_ref[2, b], 1)

    for copies in v_arrivals:
        for copy in copies:
            copy.wait()
    size = total_rows // PIECES
    for piece in range(PIECES):
        at = slice(piece * size, piece * size + size)
        product_ref[at] = dot(v_ref[at], columns)
        for b in range(piece * size // rank_size, (piece + 1) * size // rank_size):
            place(b)
    half = sum_ref.shape[0] // 2
    lane = lax.broadcasted_iota(jnp.int32, (1, 1, 128), 2)
    both = jnp.where(lane < 64, sum_ref[:half], sum_ref[half:]) + tag_ref[...]
    message_ref[...] = both.reshape(total_rows, 128).astype(BF)


def whole_vmem(count):
    return [pl.BlockSpec(memory_space=pltpu.VMEM)] * count


SCALARS = pl.BlockSpec(memory_space=pltpu.SMEM)


def stage(do_u, do_v, scalars, local, streamed, tags=()):
    steps = STEPS
    in_hbm = pl.BlockSpec(memory_space=pl.ANY)
    scratch = [pltpu.VMEM(x.shape, BF) for x in streamed]
    total_rows = streamed[-1].shape[0]
    copies = 0
    if do_u:
        copies += len(HALO) + 3 * steps
        scratch[0] = pltpu.VMEM((len(HALO),) + streamed[0].shape[2:], BF)
        scratch[4:4] = [pltpu.VMEM((5, 256, 64), BF), pltpu.VMEM((5, 256, 64), BF)]
    if do_v:
        rank_size = RANK
        out_shape = [
            jax.ShapeDtypeStruct((total_rows, 128), BF),
            jax.ShapeDtypeStruct((2, 48, 256), BF),
            jax.ShapeDtypeStruct((2, 48, 256), BF),
        ]
        out_specs = whole_vmem(3)
        scratch += [
            pltpu.VMEM((total_rows, 256), F32),
            pltpu.VMEM((2 * (total_rows // rank_size), rank_size, 128), F32),
        ]
        copies += steps
    else:
        out_shape = jax.ShapeDtypeStruct((48, 1024), F32)
        out_specs = whole_vmem(1)[0]
    return pl.pallas_call(
        functools.partial(stage_kernel, do_u, do_v, steps),
        in_specs=[SCALARS] * 3
        + whole_vmem(len(local))
        + [in_hbm] * len(streamed)
        + whole_vmem(len(tags)),
        out_specs=out_specs,
        out_shape=out_shape,
        scratch_shapes=scratch + [pltpu.SemaphoreType.DMA((copies,))],
        compiler_params=pltpu.CompilerParams(vmem_limit_bytes=STAGE_LIMIT),
        cost_estimate=pl.CostEstimate(
            flops=4_000_000_000, bytes_accessed=1_000_000, transcendentals=0
        ),
    )(*scalars, *local, *streamed, *tags)


def near_own(offsets, low, high, blocks):
    clusters = blocks.shape[0]
    return pl.pallas_call(
        near_own_kernel,
        in_specs=[SCALARS] + whole_vmem(2) + [pl.BlockSpec(memory_space=pl.ANY)],
        out_specs=whole_vmem(1)[0],
        out_shape=jax.ShapeDtypeStruct((48, clusters * 256), F32),
        scratch_shapes=[
            pltpu.VMEM(blocks.shape, BF),
            pltpu.VMEM((clusters + 1, 256, 64), BF),
            pltpu.VMEM((clusters + 1, 256, 64), BF),
            pltpu.SemaphoreType.DMA((clusters,)),
        ],
        compiler_params=pltpu.CompilerParams(vmem_limit_bytes=STAGE_LIMIT),
        cost_estimate=pl.CostEstimate(
            flops=3_000_000_000, bytes_accessed=4_500_000, transcendentals=0
        ),
    )(offsets, low, high, blocks)


def place_u(dest, far_u, count):
    return pl.pallas_call(
        place_u_kernel,
        in_specs=[SCALARS, pl.BlockSpec(memory_space=pl.ANY)],
        out_specs=pl.BlockSpec(memory_space=pltpu.VMEM),
        out_shape=jax.ShapeDtypeStruct((count, far_u.shape[2], 4 * far_u.shape[3]), BF),
        scratch_shapes=[
            pltpu.VMEM(far_u.shape, BF),
            pltpu.SMEM((count,), jnp.int32),
            pltpu.SemaphoreType.DMA,
        ],
        compiler_params=pltpu.CompilerParams(vmem_limit_bytes=SETUP_LIMIT),
    )(dest, far_u)


def on_device(
    source_field,
    near_blocks,
    near_offsets,
    far_v,
    far_u,
    far_rank,
    far_col_local,
    far_dest,
    far_row_local,
):
    parts, rhs_dev, panels_dev = source_field.shape
    rank_size = far_v.shape[2]
    count = lax.axis_size("row")
    forward = [(i, i + 1) for i in range(count - 1)]
    backward = [(i + 1, i) for i in range(count - 1)]
    core = lax.axis_index("rhs").astype(jnp.int32).reshape(1)
    dest = far_dest.reshape(-1)

    def exchange(x):
        return lax.all_to_all(x, "row", split_axis=0, concat_axis=0, tiled=True)

    u_own = exchange(place_u(dest, far_u, count))
    order = jnp.arange(dest.shape[0], dtype=jnp.int32)
    earlier = (dest[None, :] == dest[:, None]) & (order[None, :] < order[:, None])
    slot = jnp.sum(earlier.astype(jnp.int32), axis=1)
    meta = jnp.stack(
        [
            slot * count + dest,
            far_col_local // 2 * 128,
            (far_col_local % 2 != slot).astype(jnp.int32) * 64,
        ]
    )
    tag_lane = slot * 64 + 48 + far_row_local
    spread = (
        (jnp.arange(count)[:, None, None] == dest[None, None, :])
        & (jnp.arange(128)[None, :, None] == tag_lane[None, None, :])
    ).astype(F32)
    tags = [jnp.sum(spread, axis=2)[:, None, :]]
    matches = jnp.stack([near_offsets[i] == offset for i, offset in HALO])
    positions = jnp.arange(matches.shape[1], dtype=jnp.int32)
    halo = jnp.stack(
        [
            jnp.sum(jnp.where(matches, positions[None, :], 0), axis=1),
            jnp.sum(matches.astype(jnp.int32), axis=1),
        ]
    )
    scalars = [core, meta, halo]
    kept = jnp.arange(rank_size, dtype=jnp.int32)[None, :] < far_rank[:, None]
    v_rows = jnp.where(kept[:, :, None, None], far_v.transpose(0, 2, 1, 3), jnp.zeros((), BF))
    v_rows = v_rows.reshape(dest.shape[0] * rank_size, -1)
    field = source_field.reshape(parts * rhs_dev, panels_dev)
    message, low, high = stage(False, True, scalars, [field], [v_rows], tags)
    for application in range(APPS):
        left = lax.ppermute(high, "row", forward)
        right = lax.ppermute(low, "row", backward)
        arrived = exchange(message.reshape(count, rank_size, 128)).reshape(-1, 128)
        near_term = near_own(near_offsets, low, high, near_blocks)
        if application == 0:
            u_own, near_term, left, right = lax.optimization_barrier(
                (u_own, near_term, left, right)
            )
            u_own = u_own.reshape(count * rank_size, -1)
            u_other = lax.ppermute(u_own, "rhs", [(0, 1), (1, 0)])
        reach = [left, right, near_term]
        streamed = [near_blocks, arrived, u_own, u_other]
        if application < APPS - 1:
            message, low, high = stage(
                True, True, scalars, reach, streamed + [v_rows], tags
            )
    result = stage(True, False, scalars, reach, streamed)
    return result.reshape(parts, rhs_dev, panels_dev)


def solution(mesh):
    return jax.shard_map(
        on_device,
        mesh=mesh,
        in_specs=(
            P(None, "rhs", "row"),
            P("row", None, None, None, None),
            P("row", None),
            P("row", None, None, None),
            P("row", None, None, "rhs"),
            P("row"),
            P("row"),
            P("row", None),
            P("row"),
        ),
        out_specs=P(None, "rhs", "row"),
        check_vma=False,
    )
```
